512 devices in a mesh: group: 32 (over z, y_hi), blk: 16 (over y_lo, x, core).
Axes of the slice: x: 4, y: 8 (y_hi: 4, y_lo: 2; y = y_hi * 2 + y_lo), z: 8, core: 2. Of those that a mesh axis runs over, the one named last changes fastest.
Arguments:
- right_side: float32 [96, 32768], P(None, ('group', 'blk')), may hold values from -6 to 6
- positions: float32 [3, 32768], P(None, ('group', 'blk')), may hold values from -0.5 to 0.5
- wavenumber: float32 [1], replicated, may hold values from 12 to 24
Outputs:
- solution_field: float32 [96, 32768], P(None, ('group', 'blk'))
- residual: float32 [96, 32768], P(None, ('group', 'blk'))
The draws below stay inside these ranges and needn't reach their ends.
All inputs are finite; a program needn't handle non-finite values.
Results may differ from the reference program's by a relative error of at most 0.0003.
Values sent between devices are 32-bit elements; how exact they have to be, the bound alone decides.
No kernel may reach another device: no remote copies, remote signals or barrier semaphores. Data moves between devices by JAX's collectives and lax.ppermute only.
A program may use at most 64 MiB of HBM per device.

```python
import math
import jax
import jax.numpy as jnp
from jax import lax

FRAMES = 96
ITERS = 2
N_MICS = 32768


def level_of(rng, dims, pieces, least, top_value):
    def one(axis_at, shards_of):
        heights = jax.random.uniform(jax.random.fold_in(jax.random.fold_in(rng, 6), axis_at), (shards_of,), jnp.float32, least / len(pieces), top_value / len(pieces))
        return jnp.repeat(jnp.exp(heights), dims[axis_at] // shards_of).reshape((-1,) + (1,) * (len(dims) - axis_at - 1))

    level = one(*pieces[0])
    for cut in pieces[1:]:
        level = level * one(*cut)
    return level


def noise(rng, shape, spread, reach, cuts=(), dtype=jnp.bfloat16):
    array = spread * jax.random.normal(rng, shape, jnp.float32)
    if cuts:
        array = array * level_of(rng, shape, cuts, -0.22, 0.18)
    return jnp.clip(array, -reach, reach).astype(dtype)


def setup_inputs(seed: int = 0) -> dict:
    arg_keys = jax.random.split(jax.random.key(seed), 4)
    right_side = noise(arg_keys[0], (FRAMES, N_MICS), 1.0, 6.0, ((1, 512),), jnp.float32)
    positions = jnp.clip(jax.random.uniform(arg_keys[1], (3, N_MICS), jnp.float32, -0.5, 0.5) * level_of(arg_keys[1], (3, N_MICS), ((1, 512),), -0.4, 0.0), -0.5, 0.5)
    wavenumber = jnp.clip(jnp.exp(jax.random.uniform(arg_keys[2], (1,), jnp.float32, math.log(12.0), math.log(24.0))), 12.0, 24.0)
    return dict(right_side=right_side, positions=positions, wavenumber=wavenumber)


def kernel_block(cols, rows, kappa):
    delta_x = cols[0][:, None] - rows[0][None, :]
    delta_y = cols[1][:, None] - rows[1][None, :]
    delta_z = cols[2][:, None] - rows[2][None, :]
    dist = jnp.sqrt(delta_x * delta_x + delta_y * delta_y + delta_z * delta_z)
    return jnp.sinc(kappa * dist / jnp.pi)

def block_width(width):
    for cand in (512, 256, 128):
        if width % cand == 0:
            return cand
    return width

def add_columns(total, rows, cols, dirs, kappa):
    width = cols.shape[1]
    step = block_width(width)
    count = width // step

    def one_block(index, acc):
        start = (index * step).astype(jnp.int32)
        col_part = lax.dynamic_slice_in_dim(cols, start, step, 1)
        dir_part = lax.dynamic_slice_in_dim(dirs, start, step, 1)
        return acc + jnp.dot(dir_part, kernel_block(col_part, rows, kappa), preferred_element_type=jnp.float32, precision=lax.Precision.HIGHEST)
    return lax.fori_loop(0, count, one_block, total)

def reference(right_side, positions, wavenumber):
    kappa = wavenumber[0]

    def operate(field):
        empty = jnp.zeros(field.shape, jnp.float32)
        return add_columns(empty, positions, positions, field, kappa) + 0.01 * field
    solution_field = jnp.zeros_like(right_side)
    residual = right_side
    direction = right_side
    norm_now = lax.optimization_barrier(jnp.sum(residual * residual, axis=1))
    for step in range(ITERS):
        image = operate(direction)
        alpha = norm_now / lax.optimization_barrier(jnp.sum(direction * image, axis=1))
        solution_field = solution_field + alpha[:, None] * direction
        residual = residual - alpha[:, None] * image
        if step + 1 < ITERS:
            norm_next = lax.optimization_barrier(jnp.sum(residual * residual, axis=1))
            direction = residual + (norm_next / norm_now)[:, None] * direction
            norm_now = norm_next
    return (solution_field, residual)
```

```python
import math

import jax
import jax.numpy as jnp
from jax import lax
from jax.experimental import pallas as pl
from jax.experimental.pallas import tpu as pltpu
from jax.sharding import PartitionSpec as P

LANES = 128
MICS = 64
EXTRA = 8
STEP = 256
CHUNK = 128
SHIFT = 0.01
BF16 = jnp.bfloat16
F32 = jnp.float32
SINC = (
    0.9999999403953552,
    -6.579718112945557,
    12.987034797668457,
    -12.193572998046875,
    6.579925060272217,
    -1.9848603010177612,
)
PARAMS = pltpu.CompilerParams(vmem_limit_bytes=48 * 1024 * 1024)


def dot(left, right):
    return lax.dot_general(left, right, (((1,), (0,)), ((), ())), preferred_element_type=F32)


def rounded(value):
    return value.astype(BF16).astype(F32)


def lane_of(shape):
    return lax.broadcasted_iota(jnp.int32, shape, len(shape) - 1)


def frames_only(value, frames):
    return jnp.where(lane_of(value.shape) < frames, value, 0.0)


def wide(value):
    return jnp.concatenate(
        [value, jnp.zeros((value.shape[0], LANES - value.shape[1]), F32)], axis=1
    )


def halves(value):
    high = value.astype(BF16)
    return high, (value - high.astype(F32)).astype(BF16)


def start_kernel(field_ref, points_ref, wave_ref, col_ref, row_ref):
    frames = field_ref.shape[1]
    scaled = points_ref[...] * (wave_ref[0] * (0.5 / math.pi))
    squares = jnp.sum(scaled * scaled, axis=1, keepdims=True)

    def thirds(value):
        one = rounded(value)
        two = rounded(value - one)
        return one, two, rounded(value - one - two)

    rows, cols = [], []
    for axis in range(3):
        one, two, three = thirds(scaled[:, axis : axis + 1])
        rows += [one, one, two, two, one, three]
        cols += [-2.0 * v for v in (one, two, one, two, three, one)]
    rows += list(thirds(squares)) + [1.0, 1.0, 1.0]
    cols += [1.0, 1.0, 1.0] + list(thirds(squares))

    field = wide(field_ref[...])
    lane = lane_of(field.shape)
    row_block = col_block = field
    for place, (row, col) in enumerate(zip(rows, cols)):
        row_block = jnp.where(lane == frames + place, row, row_block)
        col_block = jnp.where(lane == frames + place, col, col_block)
    col_ref[...] = jnp.broadcast_to(col_block[None], col_ref.shape)
    row_ref[...] = jnp.broadcast_to(row_block[None], row_ref.shape)


def spread(out_ref, value, sums):
    out_ref[:, :MICS, :] = value.reshape(out_ref.shape[0], MICS, LANES)
    out_ref[:, MICS:, :] = jnp.broadcast_to(sums[None], (out_ref.shape[0], EXTRA, LANES))


def stacked(*rows):
    return jnp.concatenate(
        list(rows) + [jnp.zeros((EXTRA - len(rows), LANES), F32)], axis=0
    )


def product(high_ref, low_ref, weights_ref):
    both = dot(high_ref[...], weights_ref[...])
    rest = dot(low_ref[...], weights_ref[:, :LANES])
    return both[:, :LANES] + both[:, LANES:] + rest


def first_kernel(
    frames, col_ref, row_ref, field_ref, out_ref, high_ref, low_ref, weights_ref, col_f, row_f
):
    cols, rows = col_f.shape[0], row_f.shape[0]

    def factors(value):
        return jnp.where(lane_of(value.shape) < frames, 0.0, value).astype(BF16)

    def place_col(index, carry):
        at = pl.ds(pl.multiple_of(index * MICS, MICS), MICS)
        block = col_ref[index]
        col_f[at, :] = factors(block)
        high, low = halves(frames_only(block, frames))
        weights_ref[at, :LANES] = high
        weights_ref[at, LANES:] = low
        return carry

    lax.fori_loop(0, cols // MICS, place_col, 0)
    row_f[...] = factors(row_ref[...].reshape(rows, LANES))

    def columns(index, carry):
        at = pl.ds(pl.multiple_of(index * STEP, STEP), STEP)
        right = col_f[at, :]
        for first in range(0, rows, CHUNK):
            turns2 = lax.dot_general(
                row_f[first : first + CHUNK, :],
                right,
                (((1,), (1,)), ((), ())),
                preferred_element_type=F32,
            )
            turns2 = jnp.maximum(turns2, 1e-12)
            inverse = lax.rsqrt(turns2)
            turns = turns2 * inverse
            part = turns - lax.round(turns, lax.RoundingMethod.TO_NEAREST_EVEN)
            square = part * part
            value = jnp.full_like(square, SINC[-1])
            for factor in SINC[-2::-1]:
                value = value * square + factor
            high, low = halves(value * (part * inverse))
            high_ref[first : first + CHUNK, at] = high
            low_ref[first : first + CHUNK, at] = low
        return carry

    lax.fori_loop(0, cols // STEP, columns, 0)
    result = product(high_ref, low_ref, weights_ref)
    field_rows = frames_only(row_ref[...].reshape(rows, LANES), frames)
    own = field_ref[...]
    spread(
        out_ref,
        result,
        stacked(
            jnp.sum(field_rows * result, axis=0, keepdims=True),
            wide(jnp.sum(own * own, axis=0, keepdims=True)),
        ),
    )


def image_kernel(got_ref, field_ref, image_ref, send_ref):
    total = jnp.sum(got_ref[...], axis=0)
    image = total[:MICS] + SHIFT * wide(field_ref[...])
    image_ref[...] = image
    send_ref[:, :MICS, :] = jnp.broadcast_to(image[None], (send_ref.shape[0], MICS, LANES))
    send_ref[:, MICS:, :] = jnp.broadcast_to(
        total[MICS:][None], (send_ref.shape[0], EXTRA, LANES)
    )


def second_kernel(frames, got_ref, col_ref, high_ref, low_ref, out_ref, sums_ref, weights_ref):
    sums = jnp.sum(got_ref[:, MICS:, :], axis=0)
    norm = sums[1:2]
    alpha = norm / (sums[0:1] + SHIFT * norm)

    def place(index, total):
        at = pl.ds(pl.multiple_of(index * MICS, MICS), MICS)
        residual = frames_only(col_ref[index] - alpha * got_ref[index, :MICS, :], frames)
        high, low = halves(residual)
        weights_ref[at, :LANES] = high
        weights_ref[at, LANES:] = low
        return total + jnp.sum((residual * residual).reshape(-1, 8, LANES), axis=0)

    squares = lax.fori_loop(0, got_ref.shape[0], place, jnp.zeros((8, LANES), F32))
    spread(
        out_ref,
        product(high_ref, low_ref, weights_ref),
        stacked(jnp.sum(squares, axis=0, keepdims=True)),
    )
    sums_ref[...] = stacked(norm, alpha)


def direction_kernel(got_ref, field_ref, image_ref, sums_ref, keep_ref, norm_ref, send_ref):
    total = jnp.sum(got_ref[...], axis=0)
    norm, alpha, norm_next = sums_ref[0:1], sums_ref[1:2], total[MICS : MICS + 1]
    beta = norm_next / norm
    field, image = wide(field_ref[...]), image_ref[...]
    residual = field - alpha * image
    direction = residual + beta * field
    turned = total[:MICS] + SHIFT * residual + beta * image
    keep_ref[0] = alpha * field
    keep_ref[1] = residual
    keep_ref[2] = direction
    keep_ref[3] = turned
    along = jnp.sum(direction * turned, axis=0, keepdims=True)
    norm_ref[...] = stacked(norm_next)
    send_ref[...] = jnp.broadcast_to(stacked(along)[None], send_ref.shape)


def relay_kernel(got_ref, send_ref):
    total = jnp.sum(got_ref[...], axis=0)
    send_ref[...] = jnp.broadcast_to(total[None], send_ref.shape)


def end_kernel(got_ref, sums_ref, keep_ref, solution_ref, residual_ref):
    frames = solution_ref.shape[1]
    along = jnp.sum(got_ref[:, 0:1, :], axis=0)
    alpha = sums_ref[0:1] / along
    solution_ref[...] = (keep_ref[0] + alpha * keep_ref[2])[:, :frames]
    residual_ref[...] = (keep_ref[1] - alpha * keep_ref[3])[:, :frames]


def call(kernel, outs, **more):
    return pl.pallas_call(
        kernel,
        out_shape=tuple(jax.ShapeDtypeStruct(shape, dtype) for shape, dtype in outs),
        compiler_params=PARAMS,
        **more,
    )


def local(groups, blks, right_side, positions, wavenumber):
    frames = right_side.shape[0]
    field = right_side.T
    rows, cols = blks * MICS, groups * MICS
    block, summed = (MICS, LANES), (MICS + EXTRA, LANES)

    def exchange(value, axis):
        return lax.all_to_all(value, axis, 0, 0)

    scalar = pl.BlockSpec(memory_space=pltpu.SMEM)
    vector = pl.BlockSpec(memory_space=pltpu.VMEM)
    to_cols, to_rows = call(
        start_kernel,
        [((groups,) + block, F32), ((blks,) + block, F32)],
        in_specs=[vector, vector, scalar],
    )(field, positions.T, wavenumber)
    row_blocks = exchange(to_rows, "blk")
    col_blocks = exchange(to_cols, "group")

    partial, high, low = call(
        lambda *refs: first_kernel(frames, *refs),
        [((blks,) + summed, F32), ((rows, cols), BF16), ((rows, cols), BF16)],
        scratch_shapes=[
            pltpu.VMEM((cols, 2 * LANES), BF16),
            pltpu.VMEM((cols, LANES), BF16),
            pltpu.VMEM((rows, LANES), BF16),
        ],
    )(col_blocks, row_blocks, field)
    image, to_cols = call(image_kernel, [(block, F32), ((groups,) + summed, F32)])(
        exchange(partial, "blk"), field
    )
    partial, sums = call(
        lambda *refs: second_kernel(frames, *refs),
        [((blks,) + summed, F32), ((EXTRA, LANES), F32)],
        scratch_shapes=[pltpu.VMEM((cols, 2 * LANES), BF16)],
    )(exchange(to_cols, "group"), col_blocks, high, low)
    keep, norm_next, send = call(
        direction_kernel,
        [((4,) + block, F32), ((EXTRA, LANES), F32), ((blks, EXTRA, LANES), F32)],
    )(exchange(partial, "blk"), field, image, sums)
    (send,) = call(relay_kernel, [((groups, EXTRA, LANES), F32)])(exchange(send, "blk"))
    got = exchange(send, "group")
    solution_field, residual = call(
        end_kernel, [((MICS, frames), F32), ((MICS, frames), F32)]
    )(got, norm_next, keep)
    return solution_field.T, residual.T


def solution(mesh):
    groups, blks = mesh.shape["group"], mesh.shape["blk"]
    where = P(None, ("group", "blk"))
    return jax.shard_map(
        lambda *args: local(groups, blks, *args),
        mesh=mesh,
        in_specs=(where, where, P()),
        out_specs=(where, where),
        check_vma=False,
    )
```

```python
import math

import jax
import jax.numpy as jnp
from jax import lax
from jax.experimental import pallas as pl
from jax.experimental.pallas import tpu as pltpu
from jax.sharding import Mesh
from jax.sharding import PartitionSpec as P

LANES = 128
MICS = 64
FRAMES = 96
PACKED = 48
EXTRA = 8
STEP = 256
DEPTH = 64
SHIFT = 0.01
BF16 = jnp.bfloat16
F32 = jnp.float32
AXES = {"z_far": 4, "z_near": 2, "y_far": 4, "y_near": 2, "x": 4, "core": 2}
FAR, FAR_SIZE = ("z_far", "y_far"), 16
NEAR, NEAR_SIZE = ("z_near", "y_near", "x", "core"), 32
ROWS, COLS = NEAR_SIZE * MICS, FAR_SIZE * MICS
SINC = (
    0.9999999403953552,
    -6.579718112945557,
    12.987034797668457,
    -12.193572998046875,
    6.579925060272217,
    -1.9848603010177612,
)
PARAMS = pltpu.CompilerParams(vmem_limit_bytes=48 * 1024 * 1024)


def dot(left, right):
    return lax.dot_general(left, right, (((1,), (0,)), ((), ())), preferred_element_type=F32)


def rounded(value):
    return value.astype(BF16).astype(F32)


def halves(value):
    high = value.astype(BF16)
    return high, (value - high.astype(F32)).astype(BF16)


def widen(value):
    blank = jnp.zeros((value.shape[0], LANES - value.shape[1]), F32)
    return jnp.concatenate([value, blank], axis=1)


def pack(value):
    tail = value[PACKED:]
    third = FRAMES // 3
    spare = [tail[:, i * third : (i + 1) * third] for i in range(3)]
    return jnp.concatenate([value[:PACKED, :FRAMES], jnp.concatenate(spare, axis=0)], axis=1)


def unpack(block):
    spare = block[:, FRAMES:]
    tail = [spare[i * 16 : (i + 1) * 16] for i in range(3)]
    top = widen(block[:, :FRAMES])
    bottom = widen(jnp.concatenate(tail, axis=1))
    return jnp.concatenate([top, bottom], axis=0)


def rows_of(*rows):
    blank = jnp.zeros((EXTRA - len(rows), LANES), F32)
    return jnp.concatenate(list(rows) + [blank], axis=0)


def over_rows(value):
    return jnp.sum(value, axis=0, keepdims=True)


def start_kernel(field_ref, points_ref, col_ref, row_ref):
    points = points_ref[...]
    points = jnp.concatenate([points, jnp.zeros((EXTRA - 3, MICS), F32)], axis=0)
    points = widen(points)
    block = jnp.concatenate([pack(field_ref[...]), points], axis=0)
    col_ref[...] = jnp.broadcast_to(block[None], col_ref.shape)
    row_ref[...] = jnp.broadcast_to(points[None], row_ref.shape)


def factors(points, wave, of_rows):
    scaled = points * (wave * (0.5 / math.pi))
    squares = over_rows(scaled * scaled)

    def thirds(value):
        one = rounded(value)
        two = rounded(value - one)
        return one, two, rounded(value - one - two)

    one, two, three = thirds(scaled)
    ones = jnp.ones_like(squares)
    if of_rows:
        rows = [one, one, two, two, one, three]
        rest = list(thirds(squares)) + [ones] * 3
    else:
        rows = [-2.0 * v for v in (one, two, one, two, three, one)]
        rest = [ones] * 3 + list(thirds(squares))
    blank = jnp.zeros((DEPTH - 6 * EXTRA - 6, squares.shape[1]), F32)
    return jnp.concatenate(rows + rest + [blank], axis=0)


def points_of(ref, count, first):
    tiles = [ref[i, first : first + EXTRA, :MICS] for i in range(count)]
    return jnp.concatenate(tiles, axis=1)


def sinc_of(turns2):
    turns2 = jnp.maximum(turns2, 1e-12)
    inverse = lax.rsqrt(turns2)
    turns = turns2 * inverse
    part = turns - lax.round(turns, lax.RoundingMethod.TO_NEAREST_EVEN)
    square = part * part
    value = SINC[-1] * square + SINC[-2]
    for factor in SINC[-3::-1]:
        value = value * square + factor
    return value * (part * inverse)


def put_weights(weights_ref, index, value):
    at = pl.ds(pl.multiple_of(index * MICS, MICS), MICS)
    high, low = halves(value)
    weights_ref[at, :LANES] = high
    weights_ref[at, LANES:] = low


def send_rows(out_ref, index, both, rest):
    total = both[:, :LANES] + both[:, LANES:] + rest
    for i in range(STEP // MICS):
        packed = pack(total[i * MICS : (i + 1) * MICS])
        out_ref[index * (STEP // MICS) + i, :PACKED, :] = packed


def first_kernel(
    col_ref, row_ref, wave_ref, out_ref, high_ref, low_ref, weights_ref, col_f, row_f
):
    wave = wave_ref[0]

    def place(index, carry):
        put_weights(weights_ref, index, unpack(col_ref[index, :PACKED, :]))
        return carry

    lax.fori_loop(0, FAR_SIZE, place, 0)
    col_f[...] = factors(points_of(col_ref, FAR_SIZE, PACKED), wave, False).astype(BF16)
    row_f[...] = factors(points_of(row_ref, NEAR_SIZE, 0), wave, True).T.astype(BF16)

    def some_rows(index, carry):
        at = pl.ds(pl.multiple_of(index * STEP, STEP), STEP)
        left = row_f[at, :]
        both, rest = jnp.zeros((STEP, 2 * LANES), F32), jnp.zeros((STEP, LANES), F32)
        for first in range(0, COLS, STEP):
            cols = slice(first, first + STEP)
            high, low = halves(sinc_of(dot(left, col_f[:, cols])))
            high_ref[at, cols] = high
            low_ref[at, cols] = low
            both = both + dot(high, weights_ref[cols, :])
            rest = rest + dot(low, weights_ref[cols, :LANES])
        send_rows(out_ref, index, both, rest)
        return carry

    lax.fori_loop(0, ROWS // STEP, some_rows, 0)


def image_kernel(got_ref, field_ref, image_ref, send_ref):
    image = unpack(jnp.sum(got_ref[...], axis=0)) + SHIFT * widen(field_ref[...])
    image_ref[...] = image
    send_ref[...] = jnp.broadcast_to(pack(image)[None], send_ref.shape)


def second_kernel(
    got_ref, col_ref, high_ref, low_ref, out_ref, weights_ref, field_ref, image_ref
):
    def folded(value):
        return jnp.sum(value.reshape(-1, 8, LANES), axis=0)

    def place(index, sums):
        at = pl.ds(pl.multiple_of(index * MICS, MICS), MICS)
        image = unpack(got_ref[index])
        field = unpack(col_ref[index, :PACKED, :])
        put_weights(weights_ref, index, image)
        field_ref[at, :] = field
        image_ref[at, :] = image
        new = (field * field, field * image, image * image)
        return tuple(old + folded(value) for old, value in zip(sums, new))

    blank = jnp.zeros((8, LANES), F32)
    sums = lax.fori_loop(0, FAR_SIZE, place, (blank, blank, blank))
    norm, cross, square = (over_rows(value) for value in sums)
    guess = jnp.where(square > 0.0, cross / jnp.where(square > 0.0, square, 1.0), 0.0)

    def apart(index, sums):
        at = pl.ds(pl.multiple_of(index * MICS, MICS), MICS)
        image = image_ref[at, :]
        left = field_ref[at, :] - guess * image
        return sums[0] + folded(left * left), sums[1] + folded(left * image)

    sums = lax.fori_loop(0, FAR_SIZE, apart, (blank, blank))
    left_norm, left_cross = (over_rows(value) for value in sums)
    extra = rows_of(norm, cross, square, guess, left_norm, left_cross)
    out_ref[:, PACKED:, :] = jnp.broadcast_to(extra[None], (NEAR_SIZE, EXTRA, LANES))

    def some_rows(index, carry):
        at = pl.ds(pl.multiple_of(index * STEP, STEP), STEP)
        both = dot(high_ref[at, :], weights_ref[...])
        rest = dot(low_ref[at, :], weights_ref[:, :LANES])
        send_rows(out_ref, index, both, rest)
        return carry

    lax.fori_loop(0, ROWS // STEP, some_rows, 0)


def direction_kernel(got_ref, field_ref, image_ref, keep_ref, norm_ref, send_ref):
    norm, cross, square, guess, left_norm, left_cross = (
        got_ref[:, PACKED + i, :] for i in range(6)
    )
    norm = over_rows(norm)
    alpha = norm / over_rows(cross)
    off = guess - alpha
    norm_next = over_rows(left_norm + 2.0 * off * left_cross + off * off * square)
    beta = norm_next / norm
    field, image = widen(field_ref[...]), image_ref[...]
    again = unpack(jnp.sum(got_ref[:, :PACKED, :], axis=0)) + SHIFT * image
    residual = field - alpha * image
    direction = residual + beta * field
    turned = image - alpha * again + beta * image
    keep_ref[0] = alpha * field
    keep_ref[1] = residual
    keep_ref[2] = direction
    keep_ref[3] = turned
    norm_ref[...] = rows_of(norm_next)
    along = rows_of(over_rows(direction * turned))
    send_ref[...] = jnp.broadcast_to(along[None], send_ref.shape)


def relay_kernel(got_ref, send_ref):
    total = jnp.sum(got_ref[...], axis=0)
    send_ref[...] = jnp.broadcast_to(total[None], send_ref.shape)


def end_kernel(got_ref, norm_ref, keep_ref, solution_ref, residual_ref):
    along = jnp.sum(got_ref[:, 0:1, :], axis=0)
    alpha = norm_ref[0:1] / along
    solution_ref[...] = (keep_ref[0] + alpha * keep_ref[2])[:, :FRAMES]
    residual_ref[...] = (keep_ref[1] - alpha * keep_ref[3])[:, :FRAMES]


def call(kernel, outs, **more):
    return pl.pallas_call(
        kernel,
        out_shape=tuple(jax.ShapeDtypeStruct(shape, dtype) for shape, dtype in outs),
        compiler_params=PARAMS,
        **more,
    )


def local(right_side, positions, wavenumber):
    field = right_side.T
    block = (MICS, LANES)

    def exchange(value, axis):
        return lax.all_to_all(value, axis, 0, 0)

    scalar = pl.BlockSpec(memory_space=pltpu.SMEM)
    vector = pl.BlockSpec(memory_space=pltpu.VMEM)
    to_cols, to_rows = call(
        start_kernel,
        [((FAR_SIZE, PACKED + EXTRA, LANES), F32), ((NEAR_SIZE, EXTRA, LANES), F32)],
    )(field, positions)
    row_points = exchange(to_rows, NEAR)
    col_blocks = exchange(to_cols, FAR)

    partial, high, low = call(
        first_kernel,
        [((NEAR_SIZE, PACKED, LANES), F32), ((ROWS, COLS), BF16), ((ROWS, COLS), BF16)],
        in_specs=[vector, vector, scalar],
        scratch_shapes=[
            pltpu.VMEM((COLS, 2 * LANES), BF16),
            pltpu.VMEM((DEPTH, COLS), BF16),
            pltpu.VMEM((ROWS, DEPTH), BF16),
        ],
    )(col_blocks, row_points, wavenumber)
    image, to_cols = call(image_kernel, [(block, F32), ((FAR_SIZE, PACKED, LANES), F32)])(
        exchange(partial, NEAR), field
    )
    (partial,) = call(
        second_kernel,
        [((NEAR_SIZE, PACKED + EXTRA, LANES), F32)],
        scratch_shapes=[
            pltpu.VMEM((COLS, 2 * LANES), BF16),
            pltpu.VMEM((COLS, LANES), F32),
            pltpu.VMEM((COLS, LANES), F32),
        ],
    )(exchange(to_cols, FAR), col_blocks, high, low)
    keep, norm_next, send = call(
        direction_kernel,
        [((4,) + block, F32), ((EXTRA, LANES), F32), ((NEAR_SIZE, EXTRA, LANES), F32)],
    )(exchange(partial, NEAR), field, image)
    (send,) = call(relay_kernel, [((FAR_SIZE, EXTRA, LANES), F32)])(exchange(send, NEAR))
    solution_field, residual = call(
        end_kernel, [((MICS, FRAMES), F32), ((MICS, FRAMES), F32)]
    )(exchange(send, FAR), norm_next, keep)
    return solution_field.T, residual.T


def solution(mesh):
    fine = Mesh(mesh.devices.reshape(tuple(AXES.values())), tuple(AXES))
    where = P(None, tuple(AXES))
    return jax.shard_map(
        local,
        mesh=fine,
        in_specs=(where, where, P()),
        out_specs=(where, where),
        check_vma=False,
    )
```

```python
import math

import jax
import jax.numpy as jnp
from jax import lax
from jax.experimental import pallas as pl
from jax.experimental.pallas import tpu as pltpu
from jax.sharding import Mesh
from jax.sharding import PartitionSpec as P

LANES = 128
MICS = 64
FRAMES = 96
PACKED = 48
EXTRA = 8
STEP = 256
DEPTH = 64
SHIFT = 0.01
BF16 = jnp.bfloat16
F32 = jnp.float32
AXES = {"z_far": 4, "z_near": 2, "y_far": 4, "y_near": 2, "x": 4, "core": 2}
FAR, FAR_SIZE = ("z_far", "y_far"), 16
NEAR, NEAR_SIZE = ("z_near", "y_near", "x", "core"), 32
ROWS, COLS = NEAR_SIZE * MICS, FAR_SIZE * MICS
SINC = (
    0.9999999403953552,
    -6.579718112945557,
    12.987034797668457,
    -12.193572998046875,
    6.579925060272217,
    -1.9848603010177612,
)
PARAMS = pltpu.CompilerParams(vmem_limit_bytes=24 * 1024 * 1024)


def dot(left, right):
    return lax.dot_general(left, right, (((1,), (0,)), ((), ())), preferred_element_type=F32)


def rounded(value):
    return value.astype(BF16).astype(F32)


def halves(value):
    high = value.astype(BF16)
    return high, (value - high.astype(F32)).astype(BF16)


def widen(value):
    blank = jnp.zeros((value.shape[0], LANES - value.shape[1]), F32)
    return jnp.concatenate([value, blank], axis=1)


def pack(value):
    tail = value[PACKED:]
    third = FRAMES // 3
    spare = [tail[:, i * third : (i + 1) * third] for i in range(3)]
    return jnp.concatenate([value[:PACKED, :FRAMES], jnp.concatenate(spare, axis=0)], axis=1)


def unpack(block):
    spare = block[:, FRAMES:]
    tail = [spare[i * 16 : (i + 1) * 16] for i in range(3)]
    top = widen(block[:, :FRAMES])
    bottom = widen(jnp.concatenate(tail, axis=1))
    return jnp.concatenate([top, bottom], axis=0)


def rows_of(*rows):
    blank = jnp.zeros((EXTRA - len(rows), LANES), F32)
    return jnp.concatenate(list(rows) + [blank], axis=0)


def over_rows(value):
    return jnp.sum(value, axis=0, keepdims=True)


def start_kernel(field_ref, points_ref, col_ref, row_ref):
    points = points_ref[...]
    points = jnp.concatenate([points, jnp.zeros((EXTRA - 3, MICS), F32)], axis=0)
    points = widen(points)
    block = jnp.concatenate([pack(field_ref[...]), points], axis=0)
    col_ref[...] = jnp.broadcast_to(block[None], col_ref.shape)
    row_ref[...] = jnp.broadcast_to(points[None], row_ref.shape)


def factors(points, wave, of_rows):
    scaled = points * (wave * (0.5 / math.pi))
    squares = over_rows(scaled * scaled)

    def thirds(value):
        one = rounded(value)
        two = rounded(value - one)
        return one, two, rounded(value - one - two)

    one, two, three = thirds(scaled)
    ones = jnp.ones_like(squares)
    if of_rows:
        rows = [one, one, two, two, one, three]
        rest = list(thirds(squares)) + [ones] * 3
    else:
        rows = [-2.0 * v for v in (one, two, one, two, three, one)]
        rest = [ones] * 3 + list(thirds(squares))
    blank = jnp.zeros((DEPTH - 6 * EXTRA - 6, squares.shape[1]), F32)
    return jnp.concatenate(rows + rest + [blank], axis=0)


def points_of(ref, count, first):
    tiles = [ref[i, first : first + EXTRA, :MICS] for i in range(count)]
    return jnp.concatenate(tiles, axis=1)


def sinc_of(turns2):
    turns2 = jnp.maximum(turns2, 1e-12)
    inverse = lax.rsqrt(turns2)
    turns = turns2 * inverse
    part = turns - lax.round(turns, lax.RoundingMethod.TO_NEAREST_EVEN)
    square = part * part
    value = SINC[-1] * square + SINC[-2]
    for factor in SINC[-3::-1]:
        value = value * square + factor
    return value * (part * inverse)


def put_weights(weights_ref, index, value):
    at = pl.ds(pl.multiple_of(index * MICS, MICS), MICS)
    high, low = halves(value)
    weights_ref[at, :LANES] = high
    weights_ref[at, LANES:] = low


def send_rows(out_ref, index, high_ref, low_ref, weights_ref):
    at = pl.ds(pl.multiple_of(index * STEP, STEP), STEP)
    both = dot(high_ref[at, :], weights_ref[...])
    rest = dot(low_ref[at, :], weights_ref[:, :LANES])
    total = both[:, :LANES] + both[:, LANES:] + rest
    for i in range(STEP // MICS):
        packed = pack(total[i * MICS : (i + 1) * MICS])
        out_ref[index * (STEP // MICS) + i, :PACKED, :] = packed


def first_kernel(
    col_ref, row_ref, wave_ref, out_ref, high_ref, low_ref, weights_ref, col_f, row_f
):
    wave = wave_ref[0]

    def place(index, carry):
        put_weights(weights_ref, index, unpack(col_ref[index, :PACKED, :]))
        return carry

    lax.fori_loop(0, FAR_SIZE, place, 0, unroll=True)
    col_f[...] = factors(points_of(col_ref, FAR_SIZE, PACKED), wave, False).astype(BF16)
    row_f[...] = factors(points_of(row_ref, NEAR_SIZE, 0), wave, True).T.astype(BF16)

    def some_rows(index, carry):
        at = pl.ds(pl.multiple_of(index * STEP, STEP), STEP)
        left = row_f[at, :]
        for first in range(0, COLS, STEP):
            cols = slice(first, first + STEP)
            high, low = halves(sinc_of(dot(left, col_f[:, cols])))
            high_ref[at, cols] = high
            low_ref[at, cols] = low
        send_rows(out_ref, index, high_ref, low_ref, weights_ref)
        return carry

    lax.fori_loop(0, ROWS // STEP, some_rows, 0, unroll=True)


def image_kernel(got_ref, field_ref, image_ref, send_ref):
    image = unpack(jnp.sum(got_ref[...], axis=0)) + SHIFT * widen(field_ref[...])
    image_ref[...] = image
    send_ref[...] = jnp.broadcast_to(pack(image)[None], send_ref.shape)


def second_kernel(
    got_ref, col_ref, high_ref, low_ref, out_ref, weights_ref, field_ref, image_ref
):
    def folded(value):
        return jnp.sum(value.reshape(-1, 8, LANES), axis=0)

    def place(index, sums):
        at = pl.ds(pl.multiple_of(index * MICS, MICS), MICS)
        image = unpack(got_ref[index])
        field = unpack(col_ref[index, :PACKED, :])
        put_weights(weights_ref, index, image)
        field_ref[at, :] = field
        image_ref[at, :] = image
        new = (field * field, field * image, image * image)
        return tuple(old + folded(value) for old, value in zip(sums, new))

    blank = jnp.zeros((8, LANES), F32)
    sums = lax.fori_loop(0, FAR_SIZE, place, (blank, blank, blank), unroll=True)
    norm, cross, square = (over_rows(value) for value in sums)
    guess = jnp.where(square > 0.0, cross / jnp.where(square > 0.0, square, 1.0), 0.0)

    def apart(index, sums):
        at = pl.ds(pl.multiple_of(index * MICS, MICS), MICS)
        image = image_ref[at, :]
        left = field_ref[at, :] - guess * image
        return sums[0] + folded(left * left), sums[1] + folded(left * image)

    sums = lax.fori_loop(0, FAR_SIZE, apart, (blank, blank), unroll=True)
    left_norm, left_cross = (over_rows(value) for value in sums)
    extra = rows_of(norm, cross, square, guess, left_norm, left_cross)
    out_ref[:, PACKED:, :] = jnp.broadcast_to(extra[None], (NEAR_SIZE, EXTRA, LANES))

    def some_rows(index, carry):
        send_rows(out_ref, index, high_ref, low_ref, weights_ref)
        return carry

    lax.fori_loop(0, ROWS // STEP, some_rows, 0, unroll=True)


def direction_kernel(got_ref, field_ref, image_ref, keep_ref, norm_ref, send_ref):
    norm, cross, square, guess, left_norm, left_cross = (
        got_ref[:, PACKED + i, :] for i in range(6)
    )
    norm = over_rows(norm)
    alpha = norm / over_rows(cross)
    off = guess - alpha
    norm_next = over_rows(left_norm + 2.0 * off * left_cross + off * off * square)
    beta = norm_next / norm
    field, image = widen(field_ref[...]), image_ref[...]
    again = unpack(jnp.sum(got_ref[:, :PACKED, :], axis=0)) + SHIFT * image
    residual = field - alpha * image
    direction = residual + beta * field
    turned = image - alpha * again + beta * image
    keep_ref[0] = alpha * field
    keep_ref[1] = residual
    keep_ref[2] = direction
    keep_ref[3] = turned
    norm_ref[...] = rows_of(norm_next)
    along = rows_of(over_rows(direction * turned))
    send_ref[...] = jnp.broadcast_to(along[None], send_ref.shape)


def relay_kernel(got_ref, send_ref):
    total = jnp.sum(got_ref[...], axis=0)
    send_ref[...] = jnp.broadcast_to(total[None], send_ref.shape)


def end_kernel(got_ref, norm_ref, keep_ref, solution_ref, residual_ref):
    along = jnp.sum(got_ref[:, 0:1, :], axis=0)
    alpha = norm_ref[0:1] / along
    solution_ref[...] = (keep_ref[0] + alpha * keep_ref[2])[:, :FRAMES]
    residual_ref[...] = (keep_ref[1] - alpha * keep_ref[3])[:, :FRAMES]


def call(kernel, outs, **more):
    return pl.pallas_call(
        kernel,
        out_shape=tuple(jax.ShapeDtypeStruct(shape, dtype) for shape, dtype in outs),
        compiler_params=PARAMS,
        **more,
    )


def local(right_side, positions, wavenumber):
    field = right_side.T
    block = (MICS, LANES)

    def exchange(value, axis):
        return lax.all_to_all(value, axis, 0, 0)

    scalar = pl.BlockSpec(memory_space=pltpu.SMEM)
    vector = pl.BlockSpec(memory_space=pltpu.VMEM)
    to_cols, to_rows = call(
        start_kernel,
        [((FAR_SIZE, PACKED + EXTRA, LANES), F32), ((NEAR_SIZE, EXTRA, LANES), F32)],
    )(field, positions)
    row_points = exchange(to_rows, NEAR)
    col_blocks = exchange(to_cols, FAR)

    partial, high, low = call(
        first_kernel,
        [((NEAR_SIZE, PACKED, LANES), F32), ((ROWS, COLS), BF16), ((ROWS, COLS), BF16)],
        in_specs=[vector, vector, scalar],
        scratch_shapes=[
            pltpu.VMEM((COLS, 2 * LANES), BF16),
            pltpu.VMEM((DEPTH, COLS), BF16),
            pltpu.VMEM((ROWS, DEPTH), BF16),
        ],
    )(col_blocks, row_points, wavenumber)
    image, to_cols = call(image_kernel, [(block, F32), ((FAR_SIZE, PACKED, LANES), F32)])(
        exchange(partial, NEAR), field
    )
    (partial,) = call(
        second_kernel,
        [((NEAR_SIZE, PACKED + EXTRA, LANES), F32)],
        scratch_shapes=[
            pltpu.VMEM((COLS, 2 * LANES), BF16),
            pltpu.VMEM((COLS, LANES), F32),
            pltpu.VMEM((COLS, LANES), F32),
        ],
    )(exchange(to_cols, FAR), col_blocks, high, low)
    keep, norm_next, send = call(
        direction_kernel,
        [((4,) + block, F32), ((EXTRA, LANES), F32), ((NEAR_SIZE, EXTRA, LANES), F32)],
    )(exchange(partial, NEAR), field, image)
    (send,) = call(relay_kernel, [((FAR_SIZE, EXTRA, LANES), F32)])(exchange(send, NEAR))
    solution_field, residual = call(
        end_kernel, [((MICS, FRAMES), F32), ((MICS, FRAMES), F32)]
    )(exchange(send, FAR), norm_next, keep)
    return solution_field.T, residual.T


def solution(mesh):
    fine = Mesh(mesh.devices.reshape(tuple(AXES.values())), tuple(AXES))
    where = P(None, tuple(AXES))
    return jax.shard_map(
        local,
        mesh=fine,
        in_specs=(where, where, P()),
        out_specs=(where, where),
        check_vma=False,
    )
```

```python
import math

import jax
import jax.numpy as jnp
from jax import lax
from jax.experimental import pallas as pl
from jax.experimental.pallas import tpu as pltpu
from jax.sharding import Mesh
from jax.sharding import PartitionSpec as P

LANES = 128
MICS = 64
FRAMES = 96
PACKED = 48
EXTRA = 8
STEP = 256
DEPTH = 64
SHIFT = 0.01
BF16 = jnp.bfloat16
F32 = jnp.float32
AXES = {"z_far": 4, "z_near": 2, "y_far": 4, "y_near": 2, "x": 4, "core": 2}
FAR, FAR_SIZE = ("z_far", "y_far"), 16
MID, MID_SIZE = ("z_near", "y_near", "x"), 16
NEAR, NEAR_SIZE = MID + ("core",), 32
GATHERED = 2 * FAR_SIZE
ROWS, COLS = MID_SIZE * MICS, GATHERED * MICS
SINC = (
    0.9999999403953552,
    -6.579718112945557,
    12.987034797668457,
    -12.193572998046875,
    6.579925060272217,
    -1.9848603010177612,
)
PARAMS = pltpu.CompilerParams(vmem_limit_bytes=24 * 1024 * 1024)


def dot(left, right):
    return lax.dot_general(left, right, (((1,), (0,)), ((), ())), preferred_element_type=F32)


def rounded(value):
    return value.astype(BF16).astype(F32)


def halves(value):
    high = value.astype(BF16)
    return high, (value - high.astype(F32)).astype(BF16)


def widen(value):
    blank = jnp.zeros((value.shape[0], LANES - value.shape[1]), F32)
    return jnp.concatenate([value, blank], axis=1)


def pack(value):
    tail = value[PACKED:]
    third = FRAMES // 3
    spare = [tail[:, i * third : (i + 1) * third] for i in range(3)]
    return jnp.concatenate([value[:PACKED, :FRAMES], jnp.concatenate(spare, axis=0)], axis=1)


def unpack(block):
    spare = block[:, FRAMES:]
    tail = [spare[i * 16 : (i + 1) * 16] for i in range(3)]
    top = widen(block[:, :FRAMES])
    bottom = widen(jnp.concatenate(tail, axis=1))
    return jnp.concatenate([top, bottom], axis=0)


def rows_of(*rows):
    blank = jnp.zeros((EXTRA - len(rows), LANES), F32)
    return jnp.concatenate(list(rows) + [blank], axis=0)


def over_rows(value):
    return jnp.sum(value, axis=0, keepdims=True)


def start_kernel(field_ref, points_ref, col_ref, row_ref):
    points = points_ref[...]
    points = jnp.concatenate([points, jnp.zeros((EXTRA - 3, MICS), F32)], axis=0)
    points = widen(points)
    block = jnp.concatenate([pack(field_ref[...]), points], axis=0)
    col_ref[...] = jnp.broadcast_to(block[None], col_ref.shape)
    row_ref[...] = jnp.broadcast_to(points[None], row_ref.shape)


def factors(points, wave, of_rows):
    scaled = points * (wave * (0.5 / math.pi))
    squares = over_rows(scaled * scaled)

    def thirds(value):
        one = rounded(value)
        two = rounded(value - one)
        return one, two, rounded(value - one - two)

    one, two, three = thirds(scaled)
    ones = jnp.ones_like(squares)
    if of_rows:
        rows = [one, one, two, two, one, three]
        rest = list(thirds(squares)) + [ones] * 3
    else:
        rows = [-2.0 * v for v in (one, two, one, two, three, one)]
        rest = [ones] * 3 + list(thirds(squares))
    blank = jnp.zeros((DEPTH - 6 * EXTRA - 6, squares.shape[1]), F32)
    return jnp.concatenate(rows + rest + [blank], axis=0)


def points_of(ref, count, first):
    tiles = [ref[i, first : first + EXTRA, :MICS] for i in range(count)]
    return jnp.concatenate(tiles, axis=1)


def sinc_of(turns2):
    turns2 = jnp.maximum(turns2, 1e-12)
    inverse = lax.rsqrt(turns2)
    turns = turns2 * inverse
    part = turns - lax.round(turns, lax.RoundingMethod.TO_NEAREST_EVEN)
    square = part * part
    value = SINC[-1] * square + SINC[-2]
    for factor in SINC[-3::-1]:
        value = value * square + factor
    return value * (part * inverse)


def put_weights(weights_ref, index, value):
    at = pl.ds(pl.multiple_of(index * MICS, MICS), MICS)
    high, low = halves(value)
    weights_ref[at, :LANES] = high
    weights_ref[at, LANES:] = low


def send_rows(out_ref, index, high_ref, low_ref, weights_ref):
    at = pl.ds(pl.multiple_of(index * STEP, STEP), STEP)
    both = dot(high_ref[at, :], weights_ref[...])
    rest = dot(low_ref[at, :], weights_ref[:, :LANES])
    total = both[:, :LANES] + both[:, LANES:] + rest
    for i in range(STEP // MICS):
        packed = pack(total[i * MICS : (i + 1) * MICS])
        out_ref[index * (STEP // MICS) + i, :PACKED, :] = packed


def first_kernel(
    col_ref, row_ref, wave_ref, out_ref, high_ref, low_ref, weights_ref, col_f, row_f
):
    wave = wave_ref[0]

    def place(index, carry):
        put_weights(weights_ref, index, unpack(col_ref[index, :PACKED, :]))
        return carry

    lax.fori_loop(0, GATHERED, place, 0, unroll=True)
    col_f[...] = factors(points_of(col_ref, GATHERED, PACKED), wave, False).astype(BF16)
    row_f[...] = factors(points_of(row_ref, MID_SIZE, 0), wave, True).T.astype(BF16)

    def some_rows(index, carry):
        at = pl.ds(pl.multiple_of(index * STEP, STEP), STEP)
        left = row_f[at, :]
        for first in range(0, COLS, STEP):
            cols = slice(first, first + STEP)
            high, low = halves(sinc_of(dot(left, col_f[:, cols])))
            high_ref[at, cols] = high
            low_ref[at, cols] = low
        send_rows(out_ref, index, high_ref, low_ref, weights_ref)
        return carry

    lax.fori_loop(0, ROWS // STEP, some_rows, 0, unroll=True)


def image_kernel(got_ref, field_ref, image_ref, send_ref):
    image = unpack(jnp.sum(got_ref[...], axis=0)) + SHIFT * widen(field_ref[...])
    image_ref[...] = image
    send_ref[...] = jnp.broadcast_to(pack(image)[None], send_ref.shape)


def second_kernel(
    got_ref, col_ref, high_ref, low_ref, out_ref, weights_ref, field_ref, image_ref
):
    def folded(value):
        return jnp.sum(value.reshape(-1, 8, LANES), axis=0)

    def place(index, sums):
        at = pl.ds(pl.multiple_of(index * MICS, MICS), MICS)
        image = unpack(got_ref[index])
        field = unpack(col_ref[index, :PACKED, :])
        put_weights(weights_ref, index, image)
        field_ref[at, :] = field
        image_ref[at, :] = image
        new = (field * field, field * image, image * image)
        return tuple(old + folded(value) for old, value in zip(sums, new))

    blank = jnp.zeros((8, LANES), F32)
    sums = lax.fori_loop(0, GATHERED, place, (blank, blank, blank), unroll=True)
    norm, cross, square = (over_rows(value) for value in sums)
    guess = jnp.where(square > 0.0, cross / jnp.where(square > 0.0, square, 1.0), 0.0)

    def apart(index, sums):
        at = pl.ds(pl.multiple_of(index * MICS, MICS), MICS)
        image = image_ref[at, :]
        left = field_ref[at, :] - guess * image
        return sums[0] + folded(left * left), sums[1] + folded(left * image)

    sums = lax.fori_loop(0, GATHERED, apart, (blank, blank), unroll=True)
    left_norm, left_cross = (over_rows(value) for value in sums)
    extra = rows_of(norm, cross, square, guess, left_norm, left_cross)
    out_ref[:, PACKED:, :] = jnp.broadcast_to(extra[None], (MID_SIZE, EXTRA, LANES))

    def some_rows(index, carry):
        send_rows(out_ref, index, high_ref, low_ref, weights_ref)
        return carry

    lax.fori_loop(0, ROWS // STEP, some_rows, 0, unroll=True)


def direction_kernel(got_ref, field_ref, image_ref, keep_ref, norm_ref, send_ref):
    norm, cross, square, guess, left_norm, left_cross = (
        got_ref[:, PACKED + i, :] for i in range(6)
    )
    norm = over_rows(norm)
    alpha = norm / over_rows(cross)
    off = guess - alpha
    norm_next = over_rows(left_norm + 2.0 * off * left_cross + off * off * square)
    beta = norm_next / norm
    field, image = widen(field_ref[...]), image_ref[...]
    again = unpack(jnp.sum(got_ref[:, :PACKED, :], axis=0)) + SHIFT * image
    residual = field - alpha * image
    direction = residual + beta * field
    turned = image - alpha * again + beta * image
    keep_ref[0] = alpha * field
    keep_ref[1] = residual
    keep_ref[2] = direction
    keep_ref[3] = turned
    norm_ref[...] = rows_of(norm_next)
    along = rows_of(over_rows(direction * turned))
    send_ref[...] = jnp.broadcast_to(along[None], send_ref.shape)


def relay_kernel(got_ref, send_ref):
    total = jnp.sum(got_ref[...], axis=0)
    send_ref[...] = jnp.broadcast_to(total[None], send_ref.shape)


def end_kernel(got_ref, norm_ref, keep_ref, solution_ref, residual_ref):
    along = jnp.sum(got_ref[:, 0:1, :], axis=0)
    alpha = norm_ref[0:1] / along
    solution_ref[...] = (keep_ref[0] + alpha * keep_ref[2])[:, :FRAMES]
    residual_ref[...] = (keep_ref[1] - alpha * keep_ref[3])[:, :FRAMES]


def call(kernel, outs, **more):
    return pl.pallas_call(
        kernel,
        out_shape=tuple(jax.ShapeDtypeStruct(shape, dtype) for shape, dtype in outs),
        compiler_params=PARAMS,
        **more,
    )


def local(right_side, positions, wavenumber):
    field = right_side.T
    block = (MICS, LANES)

    def exchange(value, axis):
        return lax.all_to_all(value, axis, 0, 0)

    def gather(value):
        both = lax.all_gather(exchange(value, FAR), "core")
        return both.reshape((GATHERED,) + value.shape[1:])

    scalar = pl.BlockSpec(memory_space=pltpu.SMEM)
    vector = pl.BlockSpec(memory_space=pltpu.VMEM)
    to_cols, points = call(
        start_kernel,
        [((FAR_SIZE, PACKED + EXTRA, LANES), F32), ((MID_SIZE, EXTRA, LANES), F32)],
    )(field, positions)
    col_blocks = gather(to_cols)
    row_points = exchange(points, MID)

    partial, high, low = call(
        first_kernel,
        [((MID_SIZE, PACKED, LANES), F32), ((ROWS, COLS), BF16), ((ROWS, COLS), BF16)],
        in_specs=[vector, vector, scalar],
        scratch_shapes=[
            pltpu.VMEM((COLS, 2 * LANES), BF16),
            pltpu.VMEM((DEPTH, COLS), BF16),
            pltpu.VMEM((ROWS, DEPTH), BF16),
        ],
    )(col_blocks, row_points, wavenumber)
    image, to_cols = call(image_kernel, [(block, F32), ((FAR_SIZE, PACKED, LANES), F32)])(
        exchange(partial, MID), field
    )
    (partial,) = call(
        second_kernel,
        [((MID_SIZE, PACKED + EXTRA, LANES), F32)],
        scratch_shapes=[
            pltpu.VMEM((COLS, 2 * LANES), BF16),
            pltpu.VMEM((COLS, LANES), F32),
            pltpu.VMEM((COLS, LANES), F32),
        ],
    )(gather(to_cols), col_blocks, high, low)
    keep, norm_next, send = call(
        direction_kernel,
        [((4,) + block, F32), ((EXTRA, LANES), F32), ((NEAR_SIZE, EXTRA, LANES), F32)],
    )(exchange(partial, MID), field, image)
    (send,) = call(relay_kernel, [((FAR_SIZE, EXTRA, LANES), F32)])(exchange(send, NEAR))
    solution_field, residual = call(
        end_kernel, [((MICS, FRAMES), F32), ((MICS, FRAMES), F32)]
    )(exchange(send, FAR), norm_next, keep)
    return solution_field.T, residual.T


def solution(mesh):
    fine = Mesh(mesh.devices.reshape(tuple(AXES.values())), tuple(AXES))
    where = P(None, tuple(AXES))
    return jax.shard_map(
        local,
        mesh=fine,
        in_specs=(where, where, P()),
        out_specs=(where, where),
        check_vma=False,
    )
```

```python
import math

import jax
import jax.numpy as jnp
from jax import lax
from jax.experimental import pallas as pl
from jax.experimental.pallas import tpu as pltpu
from jax.sharding import Mesh
from jax.sharding import PartitionSpec as P

LANES = 128
MICS = 64
FRAMES = 96
PACKED = 48
EXTRA = 8
STEP = 256
DEPTH = 64
SHIFT = 0.01
BF16 = jnp.bfloat16
F32 = jnp.float32
AXES = {"z_far": 4, "z_near": 2, "y_far": 4, "y_near": 2, "x": 4, "core": 2}
FAR, FAR_SIZE = ("z_far", "y_far"), 16
PAIRS, PAIRS_SIZE = ("z_near", "y_near"), 4
MID, MID_SIZE = PAIRS + ("x",), 16
NEAR, NEAR_SIZE = MID + ("core",), 32
GATHERED = 2 * FAR_SIZE
ROWS, COLS = MID_SIZE * MICS, GATHERED * MICS
SINC = (
    0.9999999403953552,
    -6.579718112945557,
    12.987034797668457,
    -12.193572998046875,
    6.579925060272217,
    -1.9848603010177612,
)
PARAMS = pltpu.CompilerParams(vmem_limit_bytes=24 * 1024 * 1024)


def dot(left, right):
    return lax.dot_general(left, right, (((1,), (0,)), ((), ())), preferred_element_type=F32)


def rounded(value):
    return value.astype(BF16).astype(F32)


def halves(value):
    high = value.astype(BF16)
    return high, (value - high.astype(F32)).astype(BF16)


def widen(value):
    blank = jnp.zeros((value.shape[0], LANES - value.shape[1]), F32)
    return jnp.concatenate([value, blank], axis=1)


def pack(value):
    tail = value[PACKED:]
    third = FRAMES // 3
    spare = [tail[:, i * third : (i + 1) * third] for i in range(3)]
    return jnp.concatenate([value[:PACKED, :FRAMES], jnp.concatenate(spare, axis=0)], axis=1)


def unpack(block):
    spare = block[:, FRAMES:]
    tail = [spare[i * 16 : (i + 1) * 16] for i in range(3)]
    top = widen(block[:, :FRAMES])
    bottom = widen(jnp.concatenate(tail, axis=1))
    return jnp.concatenate([top, bottom], axis=0)


def rows_of(*rows):
    blank = jnp.zeros((EXTRA - len(rows), LANES), F32)
    return jnp.concatenate(list(rows) + [blank], axis=0)


def over_rows(value):
    return jnp.sum(value, axis=0, keepdims=True)


def start_kernel(field_ref, points_ref, col_ref, row_ref):
    points = points_ref[...]
    points = jnp.concatenate([points, jnp.zeros((EXTRA - 3, MICS), F32)], axis=0)
    points = widen(points)
    block = jnp.concatenate([pack(field_ref[...]), points], axis=0)
    col_ref[...] = jnp.broadcast_to(block[None], col_ref.shape)
    row_ref[...] = points


def factors(points, wave, of_rows):
    scaled = points * (wave * (0.5 / math.pi))
    squares = over_rows(scaled * scaled)

    def thirds(value):
        one = rounded(value)
        two = rounded(value - one)
        return one, two, rounded(value - one - two)

    one, two, three = thirds(scaled)
    ones = jnp.ones_like(squares)
    if of_rows:
        rows = [one, one, two, two, one, three]
        rest = list(thirds(squares)) + [ones] * 3
    else:
        rows = [-2.0 * v for v in (one, two, one, two, three, one)]
        rest = [ones] * 3 + list(thirds(squares))
    blank = jnp.zeros((DEPTH - 6 * EXTRA - 6, squares.shape[1]), F32)
    return jnp.concatenate(rows + rest + [blank], axis=0)


def side_by_side(tiles):
    return jnp.concatenate([tile[:, :MICS] for tile in tiles], axis=1)


def sinc_of(turns2):
    turns2 = jnp.maximum(turns2, 1e-12)
    inverse = lax.rsqrt(turns2)
    turns = turns2 * inverse
    part = turns - lax.round(turns, lax.RoundingMethod.TO_NEAREST_EVEN)
    square = part * part
    value = SINC[-1] * square + SINC[-2]
    for factor in SINC[-3::-1]:
        value = value * square + factor
    return value * (part * inverse)


def put_weights(weights_ref, index, value):
    at = pl.ds(pl.multiple_of(index * MICS, MICS), MICS)
    high, low = halves(value)
    weights_ref[at, :LANES] = high
    weights_ref[at, LANES:] = low


def send_rows(out_ref, index, high_ref, low_ref, weights_ref):
    at = pl.ds(pl.multiple_of(index * STEP, STEP), STEP)
    both = dot(high_ref[at, :], weights_ref[...])
    rest = dot(low_ref[at, :], weights_ref[:, :LANES])
    total = both[:, :LANES] + both[:, LANES:] + rest
    for i in range(STEP // MICS):
        packed = pack(total[i * MICS : (i + 1) * MICS])
        out_ref[index * (STEP // MICS) + i, :PACKED, :] = packed


def first_kernel(
    col_ref,
    row_ref,
    row1_ref,
    row2_ref,
    row3_ref,
    place_ref,
    wave_ref,
    out_ref,
    high_ref,
    low_ref,
    weights_ref,
    col_f,
    row_f,
    tiles_ref,
):
    wave = wave_ref[0]

    def place(index, carry):
        put_weights(weights_ref, index, unpack(col_ref[index, :PACKED, :]))
        return carry

    lax.fori_loop(0, GATHERED, place, 0, unroll=True)
    cols = side_by_side([col_ref[i, PACKED:, :] for i in range(GATHERED)])
    col_f[...] = factors(cols, wave, False).astype(BF16)
    for i, ref in enumerate((row_ref, row1_ref, row2_ref, row3_ref)):
        tiles_ref[i * PAIRS_SIZE : (i + 1) * PAIRS_SIZE] = ref[...]
    rows = side_by_side([tiles_ref[place_ref[i]] for i in range(MID_SIZE)])
    row_f[...] = factors(rows, wave, True).T.astype(BF16)

    def some_rows(index, carry):
        at = pl.ds(pl.multiple_of(index * STEP, STEP), STEP)
        left = row_f[at, :]
        for first in range(0, COLS, STEP):
            cols = slice(first, first + STEP)
            high, low = halves(sinc_of(dot(left, col_f[:, cols])))
            high_ref[at, cols] = high
            low_ref[at, cols] = low
        send_rows(out_ref, index, high_ref, low_ref, weights_ref)
        return carry

    lax.fori_loop(0, ROWS // STEP, some_rows, 0, unroll=True)


def image_kernel(got_ref, field_ref, image_ref, send_ref):
    image = unpack(jnp.sum(got_ref[...], axis=0)) + SHIFT * widen(field_ref[...])
    image_ref[...] = image
    send_ref[...] = jnp.broadcast_to(pack(image)[None], send_ref.shape)


def second_kernel(
    got_ref, col_ref, high_ref, low_ref, out_ref, weights_ref, field_ref, image_ref
):
    def folded(value):
        return jnp.sum(value.reshape(-1, 8, LANES), axis=0)

    def place(index, sums):
        at = pl.ds(pl.multiple_of(index * MICS, MICS), MICS)
        image = unpack(got_ref[index])
        field = unpack(col_ref[index, :PACKED, :])
        put_weights(weights_ref, index, image)
        field_ref[at, :] = field
        image_ref[at, :] = image
        new = (field * field, field * image, image * image)
        return tuple(old + folded(value) for old, value in zip(sums, new))

    blank = jnp.zeros((8, LANES), F32)
    sums = lax.fori_loop(0, GATHERED, place, (blank, blank, blank), unroll=True)
    norm, cross, square = (over_rows(value) for value in sums)
    guess = jnp.where(square > 0.0, cross / jnp.where(square > 0.0, square, 1.0), 0.0)

    def apart(index, sums):
        at = pl.ds(pl.multiple_of(index * MICS, MICS), MICS)
        image = image_ref[at, :]
        left = field_ref[at, :] - guess * image
        return sums[0] + folded(left * left), sums[1] + folded(left * image)

    sums = lax.fori_loop(0, GATHERED, apart, (blank, blank), unroll=True)
    left_norm, left_cross = (over_rows(value) for value in sums)
    extra = rows_of(norm, cross, square, guess, left_norm, left_cross)
    out_ref[:, PACKED:, :] = jnp.broadcast_to(extra[None], (MID_SIZE, EXTRA, LANES))

    def some_rows(index, carry):
        send_rows(out_ref, index, high_ref, low_ref, weights_ref)
        return carry

    lax.fori_loop(0, ROWS // STEP, some_rows, 0, unroll=True)


def direction_kernel(got_ref, field_ref, image_ref, keep_ref, norm_ref, send_ref):
    norm, cross, square, guess, left_norm, left_cross = (
        got_ref[:, PACKED + i, :] for i in range(6)
    )
    norm = over_rows(norm)
    alpha = norm / over_rows(cross)
    off = guess - alpha
    norm_next = over_rows(left_norm + 2.0 * off * left_cross + off * off * square)
    beta = norm_next / norm
    field, image = widen(field_ref[...]), image_ref[...]
    again = unpack(jnp.sum(got_ref[:, :PACKED, :], axis=0)) + SHIFT * image
    residual = field - alpha * image
    direction = residual + beta * field
    turned = image - alpha * again + beta * image
    keep_ref[0] = alpha * field
    keep_ref[1] = residual
    keep_ref[2] = direction
    keep_ref[3] = turned
    norm_ref[...] = rows_of(norm_next)
    along = over_rows(direction * turned)
    send_ref[...] = jnp.broadcast_to(along[None], send_ref.shape)


def relay_kernel(got_ref, send_ref):
    total = jnp.sum(got_ref[...], axis=0)
    send_ref[...] = jnp.broadcast_to(total[None], send_ref.shape)


def end_kernel(got_ref, norm_ref, keep_ref, solution_ref, residual_ref):
    along = jnp.sum(got_ref[...], axis=0)
    alpha = norm_ref[0:1] / along
    solution_ref[...] = (keep_ref[0] + alpha * keep_ref[2])[:, :FRAMES]
    residual_ref[...] = (keep_ref[1] - alpha * keep_ref[3])[:, :FRAMES]


def call(kernel, outs, **more):
    return pl.pallas_call(
        kernel,
        out_shape=tuple(jax.ShapeDtypeStruct(shape, dtype) for shape, dtype in outs),
        compiler_params=PARAMS,
        **more,
    )


def points_of_mid(points):
    pair = 2 * lax.axis_index("z_near") + lax.axis_index("y_near")
    column = lax.axis_index("x")
    columns = AXES["x"]

    def across(value, bits):
        return lax.ppermute(value, PAIRS, [(i, i ^ bits) for i in range(PAIRS_SIZE)])

    def along(value, step):
        return lax.ppermute(value, "x", [(i, (i + step) % columns) for i in range(columns)])

    four = jnp.stack([points] + [across(points, bits) for bits in range(1, PAIRS_SIZE)])
    every = [four] + [along(four, step) for step in range(1, columns)]
    index = lax.iota(jnp.int32, MID_SIZE)
    back = (column - index % columns) % columns
    return *every, back * PAIRS_SIZE + ((index // columns) ^ pair)


def local(right_side, positions, wavenumber):
    field = right_side.T
    block = (MICS, LANES)

    def exchange(value, axis):
        return lax.all_to_all(value, axis, 0, 0)

    def gather(value):
        both = lax.all_gather(exchange(value, FAR), "core")
        return both.reshape((GATHERED,) + value.shape[1:])

    scalar = pl.BlockSpec(memory_space=pltpu.SMEM)
    vector = pl.BlockSpec(memory_space=pltpu.VMEM)
    to_cols, points = call(
        start_kernel,
        [((FAR_SIZE, PACKED + EXTRA, LANES), F32), ((EXTRA, LANES), F32)],
    )(field, positions)
    col_blocks = gather(to_cols)
    row_points = points_of_mid(points)

    partial, high, low = call(
        first_kernel,
        [((MID_SIZE, PACKED, LANES), F32), ((ROWS, COLS), BF16), ((ROWS, COLS), BF16)],
        in_specs=[vector] * 5 + [scalar] * 2,
        scratch_shapes=[
            pltpu.VMEM((COLS, 2 * LANES), BF16),
            pltpu.VMEM((DEPTH, COLS), BF16),
            pltpu.VMEM((ROWS, DEPTH), BF16),
            pltpu.VMEM((MID_SIZE, EXTRA, LANES), F32),
        ],
    )(col_blocks, *row_points, wavenumber)
    image, to_cols = call(image_kernel, [(block, F32), ((FAR_SIZE, PACKED, LANES), F32)])(
        exchange(partial, MID), field
    )
    (partial,) = call(
        second_kernel,
        [((MID_SIZE, PACKED + EXTRA, LANES), F32)],
        scratch_shapes=[
            pltpu.VMEM((COLS, 2 * LANES), BF16),
            pltpu.VMEM((COLS, LANES), F32),
            pltpu.VMEM((COLS, LANES), F32),
        ],
    )(gather(to_cols), col_blocks, high, low)
    keep, norm_next, send = call(
        direction_kernel,
        [((4,) + block, F32), ((EXTRA, LANES), F32), ((NEAR_SIZE, 1, LANES), F32)],
    )(exchange(partial, MID), field, image)
    (send,) = call(relay_kernel, [((FAR_SIZE, 1, LANES), F32)])(exchange(send, NEAR))
    solution_field, residual = call(
        end_kernel, [((MICS, FRAMES), F32), ((MICS, FRAMES), F32)]
    )(exchange(send, FAR), norm_next, keep)
    return solution_field.T, residual.T


def solution(mesh):
    fine = Mesh(mesh.devices.reshape(tuple(AXES.values())), tuple(AXES))
    where = P(None, tuple(AXES))
    return jax.shard_map(
        local,
        mesh=fine,
        in_specs=(where, where, P()),
        out_specs=(where, where),
        check_vma=False,
    )
```

```python
import math

import jax
import jax.numpy as jnp
from jax import lax
from jax.experimental import pallas as pl
from jax.experimental.pallas import tpu as pltpu
from jax.sharding import Mesh
from jax.sharding import PartitionSpec as P

LANES = 128
MICS = 64
FRAMES = 96
PACKED = 48
EXTRA = 8
STEP = 256
DEPTH = 64
SHIFT = 0.01
BF16 = jnp.bfloat16
F32 = jnp.float32
AXES = {"z_far": 4, "z_near": 2, "y_far": 4, "y_near": 2, "x": 4, "core": 2}
FAR, FAR_SIZE = ("z_far", "y_far"), 16
MID, MID_SIZE = ("z_near", "y_near", "x"), 16
FIRST, FIRST_SIZE = ("z_far", "z_near", "core"), 16
LAST, LAST_SIZE = ("y_far", "y_near", "x"), 32
GATHERED = 2 * FAR_SIZE
ROWS, COLS = MID_SIZE * MICS, GATHERED * MICS
SINC = (
    0.9999999403953552,
    -6.579718112945557,
    12.987034797668457,
    -12.193572998046875,
    6.579925060272217,
    -1.9848603010177612,
)
PARAMS = pltpu.CompilerParams(vmem_limit_bytes=24 * 1024 * 1024)


def dot(left, right):
    return lax.dot_general(left, right, (((1,), (0,)), ((), ())), preferred_element_type=F32)


def rounded(value):
    return value.astype(BF16).astype(F32)


def halves(value):
    high = value.astype(BF16)
    return high, (value - high.astype(F32)).astype(BF16)


def widen(value):
    blank = jnp.zeros((value.shape[0], LANES - value.shape[1]), F32)
    return jnp.concatenate([value, blank], axis=1)


def pack(value):
    tail = value[PACKED:]
    third = FRAMES // 3
    spare = [tail[:, i * third : (i + 1) * third] for i in range(3)]
    return jnp.concatenate([value[:PACKED, :FRAMES], jnp.concatenate(spare, axis=0)], axis=1)


def unpack(block):
    spare = block[:, FRAMES:]
    tail = [spare[i * 16 : (i + 1) * 16] for i in range(3)]
    top = widen(block[:, :FRAMES])
    bottom = widen(jnp.concatenate(tail, axis=1))
    return jnp.concatenate([top, bottom], axis=0)


def rows_of(*rows):
    blank = jnp.zeros((EXTRA - len(rows), LANES), F32)
    return jnp.concatenate(list(rows) + [blank], axis=0)


def over_rows(value):
    return jnp.sum(value, axis=0, keepdims=True)


def start_kernel(field_ref, points_ref, col_ref, row_ref):
    points = points_ref[...]
    points = jnp.concatenate([points, jnp.zeros((EXTRA - 3, MICS), F32)], axis=0)
    points = widen(points)
    block = jnp.concatenate([pack(field_ref[...]), points], axis=0)
    col_ref[...] = jnp.broadcast_to(block[None], col_ref.shape)
    row_ref[...] = jnp.broadcast_to(points[None], row_ref.shape)


def factors(points, wave, of_rows):
    scaled = points * (wave * (0.5 / math.pi))
    squares = over_rows(scaled * scaled)

    def thirds(value):
        one = rounded(value)
        two = rounded(value - one)
        return one, two, rounded(value - one - two)

    one, two, three = thirds(scaled)
    ones = jnp.ones_like(squares)
    if of_rows:
        rows = [one, one, two, two, one, three]
        rest = list(thirds(squares)) + [ones] * 3
    else:
        rows = [-2.0 * v for v in (one, two, one, two, three, one)]
        rest = [ones] * 3 + list(thirds(squares))
    blank = jnp.zeros((DEPTH - 6 * EXTRA - 6, squares.shape[1]), F32)
    return jnp.concatenate(rows + rest + [blank], axis=0)


def points_of(ref, count, first):
    tiles = [ref[i, first : first + EXTRA, :MICS] for i in range(count)]
    return jnp.concatenate(tiles, axis=1)


def sinc_of(turns2):
    turns2 = jnp.maximum(turns2, 1e-12)
    inverse = lax.rsqrt(turns2)
    turns = turns2 * inverse
    part = turns - lax.round(turns, lax.RoundingMethod.TO_NEAREST_EVEN)
    square = part * part
    value = SINC[-1] * square + SINC[-2]
    for factor in SINC[-3::-1]:
        value = value * square + factor
    return value * (part * inverse)


def put_weights(weights_ref, index, value):
    at = pl.ds(pl.multiple_of(index * MICS, MICS), MICS)
    high, low = halves(value)
    weights_ref[at, :LANES] = high
    weights_ref[at, LANES:] = low


def send_rows(out_ref, index, high_ref, low_ref, weights_ref):
    at = pl.ds(pl.multiple_of(index * STEP, STEP), STEP)
    both = dot(high_ref[at, :], weights_ref[...])
    rest = dot(low_ref[at, :], weights_ref[:, :LANES])
    total = both[:, :LANES] + both[:, LANES:] + rest
    for i in range(STEP // MICS):
        packed = pack(total[i * MICS : (i + 1) * MICS])
        out_ref[index * (STEP // MICS) + i, :PACKED, :] = packed


def first_kernel(
    col_ref, row_ref, wave_ref, out_ref, high_ref, low_ref, weights_ref, col_f, row_f
):
    wave = wave_ref[0]

    def place(index, carry):
        put_weights(weights_ref, index, unpack(col_ref[index, :PACKED, :]))
        return carry

    lax.fori_loop(0, GATHERED, place, 0, unroll=True)
    col_f[...] = factors(points_of(col_ref, GATHERED, PACKED), wave, False).astype(BF16)
    row_f[...] = factors(points_of(row_ref, MID_SIZE, 0), wave, True).T.astype(BF16)

    def some_rows(index, carry):
        at = pl.ds(pl.multiple_of(index * STEP, STEP), STEP)
        left = row_f[at, :]
        for first in range(0, COLS, STEP):
            cols = slice(first, first + STEP)
            high, low = halves(sinc_of(dot(left, col_f[:, cols])))
            high_ref[at, cols] = high
            low_ref[at, cols] = low
        send_rows(out_ref, index, high_ref, low_ref, weights_ref)
        return carry

    lax.fori_loop(0, ROWS // STEP, some_rows, 0, unroll=True)


def image_kernel(got_ref, field_ref, image_ref, send_ref):
    image = unpack(jnp.sum(got_ref[...], axis=0)) + SHIFT * widen(field_ref[...])
    image_ref[...] = image
    send_ref[...] = jnp.broadcast_to(pack(image)[None], send_ref.shape)


def second_kernel(
    got_ref, col_ref, high_ref, low_ref, out_ref, weights_ref, field_ref, image_ref
):
    def folded(value):
        return jnp.sum(value.reshape(-1, 8, LANES), axis=0)

    def place(index, sums):
        at = pl.ds(pl.multiple_of(index * MICS, MICS), MICS)
        image = unpack(got_ref[index])
        field = unpack(col_ref[index, :PACKED, :])
        put_weights(weights_ref, index, image)
        field_ref[at, :] = field
        image_ref[at, :] = image
        new = (field * field, field * image, image * image)
        return tuple(old + folded(value) for old, value in zip(sums, new))

    blank = jnp.zeros((8, LANES), F32)
    sums = lax.fori_loop(0, GATHERED, place, (blank, blank, blank), unroll=True)
    norm, cross, square = (over_rows(value) for value in sums)
    guess = jnp.where(square > 0.0, cross / jnp.where(square > 0.0, square, 1.0), 0.0)

    def apart(index, sums):
        at = pl.ds(pl.multiple_of(index * MICS, MICS), MICS)
        image = image_ref[at, :]
        left = field_ref[at, :] - guess * image
        return sums[0] + folded(left * left), sums[1] + folded(left * image)

    sums = lax.fori_loop(0, GATHERED, apart, (blank, blank), unroll=True)
    left_norm, left_cross = (over_rows(value) for value in sums)
    extra = rows_of(norm, cross, square, guess, left_norm, left_cross)
    out_ref[:, PACKED:, :] = jnp.broadcast_to(extra[None], (MID_SIZE, EXTRA, LANES))

    def some_rows(index, carry):
        send_rows(out_ref, index, high_ref, low_ref, weights_ref)
        return carry

    lax.fori_loop(0, ROWS // STEP, some_rows, 0, unroll=True)


def direction_kernel(got_ref, field_ref, image_ref, keep_ref, norm_ref, send_ref):
    norm, cross, square, guess, left_norm, left_cross = (
        got_ref[:, PACKED + i, :] for i in range(6)
    )
    norm = over_rows(norm)
    alpha = norm / over_rows(cross)
    off = guess - alpha
    norm_next = over_rows(left_norm + 2.0 * off * left_cross + off * off * square)
    beta = norm_next / norm
    field, image = widen(field_ref[...]), image_ref[...]
    again = unpack(jnp.sum(got_ref[:, :PACKED, :], axis=0)) + SHIFT * image
    residual = field - alpha * image
    direction = residual + beta * field
    turned = image - alpha * again + beta * image
    keep_ref[0] = alpha * field
    keep_ref[1] = residual
    keep_ref[2] = direction
    keep_ref[3] = turned
    norm_ref[...] = rows_of(norm_next)
    along = over_rows(direction * turned)
    send_ref[...] = jnp.broadcast_to(along[None], send_ref.shape)


def relay_kernel(got_ref, send_ref):
    total = jnp.sum(got_ref[...], axis=0)
    send_ref[...] = jnp.broadcast_to(total[None], send_ref.shape)


def end_kernel(got_ref, norm_ref, keep_ref, solution_ref, residual_ref):
    along = jnp.sum(got_ref[...], axis=0)
    alpha = norm_ref[0:1] / along
    solution_ref[...] = (keep_ref[0] + alpha * keep_ref[2])[:, :FRAMES]
    residual_ref[...] = (keep_ref[1] - alpha * keep_ref[3])[:, :FRAMES]


def call(kernel, outs, **more):
    return pl.pallas_call(
        kernel,
        out_shape=tuple(jax.ShapeDtypeStruct(shape, dtype) for shape, dtype in outs),
        compiler_params=PARAMS,
        **more,
    )


def local(right_side, positions, wavenumber):
    field = right_side.T
    block = (MICS, LANES)

    def exchange(value, axis):
        return lax.all_to_all(value, axis, 0, 0)

    def gather(value):
        both = lax.all_gather(exchange(value, FAR), "core")
        return both.reshape((GATHERED,) + value.shape[1:])

    scalar = pl.BlockSpec(memory_space=pltpu.SMEM)
    vector = pl.BlockSpec(memory_space=pltpu.VMEM)
    to_cols, points = call(
        start_kernel,
        [((FAR_SIZE, PACKED + EXTRA, LANES), F32), ((MID_SIZE, EXTRA, LANES), F32)],
    )(field, positions)
    col_blocks = gather(to_cols)
    row_points = exchange(points, MID)

    partial, high, low = call(
        first_kernel,
        [((MID_SIZE, PACKED, LANES), F32), ((ROWS, COLS), BF16), ((ROWS, COLS), BF16)],
        in_specs=[vector, vector, scalar],
        scratch_shapes=[
            pltpu.VMEM((COLS, 2 * LANES), BF16),
            pltpu.VMEM((DEPTH, COLS), BF16),
            pltpu.VMEM((ROWS, DEPTH), BF16),
        ],
    )(col_blocks, row_points, wavenumber)
    image, to_cols = call(image_kernel, [(block, F32), ((FAR_SIZE, PACKED, LANES), F32)])(
        exchange(partial, MID), field
    )
    (partial,) = call(
        second_kernel,
        [((MID_SIZE, PACKED + EXTRA, LANES), F32)],
        scratch_shapes=[
            pltpu.VMEM((COLS, 2 * LANES), BF16),
            pltpu.VMEM((COLS, LANES), F32),
            pltpu.VMEM((COLS, LANES), F32),
        ],
    )(gather(to_cols), col_blocks, high, low)
    keep, norm_next, send = call(
        direction_kernel,
        [((4,) + block, F32), ((EXTRA, LANES), F32), ((FIRST_SIZE, 1, LANES), F32)],
    )(exchange(partial, MID), field, image)
    (send,) = call(relay_kernel, [((LAST_SIZE, 1, LANES), F32)])(exchange(send, FIRST))
    solution_field, residual = call(
        end_kernel, [((MICS, FRAMES), F32), ((MICS, FRAMES), F32)]
    )(exchange(send, LAST), norm_next, keep)
    return solution_field.T, residual.T


def solution(mesh):
    fine = Mesh(mesh.devices.reshape(tuple(AXES.values())), tuple(AXES))
    where = P(None, tuple(AXES))
    return jax.shard_map(
        local,
        mesh=fine,
        in_specs=(where, where, P()),
        out_specs=(where, where),
        check_vma=False,
    )
```

```python
import math

import jax
import jax.numpy as jnp
import numpy as np
from jax import lax
from jax.experimental import pallas as pl
from jax.experimental.pallas import tpu as pltpu
from jax.sharding import Mesh
from jax.sharding import PartitionSpec as P

LANES = 128
MICS = 64
FRAMES = 96
PACKED = 48
EXTRA = 8
STEP = 256
DEPTH = 64
SHIFT = 0.01
BF16 = jnp.bfloat16
F32 = jnp.float32
AXES = {"z_far": 4, "z_near": 2, "y_far": 4, "y_near": 2, "x": 4, "core": 2}
FAR, FAR_SIZE = {"z_far": 2, "y_far": 2}, 16
MID, MID_SIZE = {"z_near": 0, "y_near": 0, "x": 2}, 16
FIRST, FIRST_SIZE = {"z_far": 2, "z_near": 0, "core": 0}, 16
LAST, LAST_SIZE = {"y_far": 2, "y_near": 0, "x": 2}, 32
GATHERED = 2 * FAR_SIZE
ROWS, COLS = MID_SIZE * MICS, GATHERED * MICS
SINC = (
    0.9999999403953552,
    -6.579718112945557,
    12.987034797668457,
    -12.193572998046875,
    6.579925060272217,
    -1.9848603010177612,
)
PARAMS = pltpu.CompilerParams(vmem_limit_bytes=24 * 1024 * 1024)


def groups_of(axes):
    places = np.arange(math.prod(AXES.values())).reshape(tuple(AXES.values()))
    names = list(AXES)
    for name, first in axes.items():
        places = np.roll(places, -first, names.index(name))
    members = math.prod(AXES[name] for name in axes)
    places = np.moveaxis(places, [names.index(name) for name in axes], range(-len(axes), 0))
    return places.reshape(-1, members).tolist()


def dot(left, right):
    return lax.dot_general(left, right, (((1,), (0,)), ((), ())), preferred_element_type=F32)


def rounded(value):
    return value.astype(BF16).astype(F32)


def halves(value):
    high = value.astype(BF16)
    return high, (value - high.astype(F32)).astype(BF16)


def widen(value):
    blank = jnp.zeros((value.shape[0], LANES - value.shape[1]), F32)
    return jnp.concatenate([value, blank], axis=1)


def pack(value):
    tail = value[PACKED:]
    third = FRAMES // 3
    spare = [tail[:, i * third : (i + 1) * third] for i in range(3)]
    return jnp.concatenate([value[:PACKED, :FRAMES], jnp.concatenate(spare, axis=0)], axis=1)


def unpack(block):
    spare = block[:, FRAMES:]
    tail = [spare[i * 16 : (i + 1) * 16] for i in range(3)]
    top = widen(block[:, :FRAMES])
    bottom = widen(jnp.concatenate(tail, axis=1))
    return jnp.concatenate([top, bottom], axis=0)


def rows_of(*rows):
    blank = jnp.zeros((EXTRA - len(rows), LANES), F32)
    return jnp.concatenate(list(rows) + [blank], axis=0)


def over_rows(value):
    return jnp.sum(value, axis=0, keepdims=True)


def start_kernel(field_ref, points_ref, col_ref, row_ref):
    points = points_ref[...]
    points = jnp.concatenate([points, jnp.zeros((EXTRA - 3, MICS), F32)], axis=0)
    points = widen(points)
    block = jnp.concatenate([pack(field_ref[...]), points], axis=0)
    col_ref[...] = jnp.broadcast_to(block[None], col_ref.shape)
    row_ref[...] = jnp.broadcast_to(points[None], row_ref.shape)


def factors(points, wave, of_rows):
    scaled = points * (wave * (0.5 / math.pi))
    squares = over_rows(scaled * scaled)

    def thirds(value):
        one = rounded(value)
        two = rounded(value - one)
        return one, two, rounded(value - one - two)

    one, two, three = thirds(scaled)
    ones = jnp.ones_like(squares)
    if of_rows:
        rows = [one, one, two, two, one, three]
        rest = list(thirds(squares)) + [ones] * 3
    else:
        rows = [-2.0 * v for v in (one, two, one, two, three, one)]
        rest = [ones] * 3 + list(thirds(squares))
    blank = jnp.zeros((DEPTH - 6 * EXTRA - 6, squares.shape[1]), F32)
    return jnp.concatenate(rows + rest + [blank], axis=0)


def points_of(ref, count, first):
    tiles = [ref[i, first : first + EXTRA, :MICS] for i in range(count)]
    return jnp.concatenate(tiles, axis=1)


def sinc_of(turns2):
    turns2 = jnp.maximum(turns2, 1e-12)
    inverse = lax.rsqrt(turns2)
    turns = turns2 * inverse
    part = turns - lax.round(turns, lax.RoundingMethod.TO_NEAREST_EVEN)
    square = part * part
    value = SINC[-1] * square + SINC[-2]
    for factor in SINC[-3::-1]:
        value = value * square + factor
    return value * (part * inverse)


def put_weights(weights_ref, index, value):
    at = pl.ds(pl.multiple_of(index * MICS, MICS), MICS)
    high, low = halves(value)
    weights_ref[at, :LANES] = high
    weights_ref[at, LANES:] = low


def send_rows(out_ref, index, high_ref, low_ref, weights_ref):
    at = pl.ds(pl.multiple_of(index * STEP, STEP), STEP)
    both = dot(high_ref[at, :], weights_ref[...])
    rest = dot(low_ref[at, :], weights_ref[:, :LANES])
    total = both[:, :LANES] + both[:, LANES:] + rest
    for i in range(STEP // MICS):
        packed = pack(total[i * MICS : (i + 1) * MICS])
        out_ref[index * (STEP // MICS) + i, :PACKED, :] = packed


def first_kernel(
    col_ref, row_ref, wave_ref, out_ref, high_ref, low_ref, weights_ref, col_f, row_f
):
    wave = wave_ref[0]

    def place(index, carry):
        put_weights(weights_ref, index, unpack(col_ref[index, :PACKED, :]))
        return carry

    lax.fori_loop(0, GATHERED, place, 0, unroll=True)
    col_f[...] = factors(points_of(col_ref, GATHERED, PACKED), wave, False).astype(BF16)
    row_f[...] = factors(points_of(row_ref, MID_SIZE, 0), wave, True).T.astype(BF16)

    def some_rows(index, carry):
        at = pl.ds(pl.multiple_of(index * STEP, STEP), STEP)
        left = row_f[at, :]
        for first in range(0, COLS, STEP):
            cols = slice(first, first + STEP)
            high, low = halves(sinc_of(dot(left, col_f[:, cols])))
            high_ref[at, cols] = high
            low_ref[at, cols] = low
        send_rows(out_ref, index, high_ref, low_ref, weights_ref)
        return carry

    lax.fori_loop(0, ROWS // STEP, some_rows, 0, unroll=True)


def image_kernel(got_ref, field_ref, image_ref, send_ref):
    image = unpack(jnp.sum(got_ref[...], axis=0)) + SHIFT * widen(field_ref[...])
    image_ref[...] = image
    send_ref[...] = jnp.broadcast_to(pack(image)[None], send_ref.shape)


def second_kernel(
    got_ref, col_ref, high_ref, low_ref, out_ref, weights_ref, field_ref, image_ref
):
    def folded(value):
        return jnp.sum(value.reshape(-1, 8, LANES), axis=0)

    def place(index, sums):
        at = pl.ds(pl.multiple_of(index * MICS, MICS), MICS)
        image = unpack(got_ref[index])
        field = unpack(col_ref[index, :PACKED, :])
        put_weights(weights_ref, index, image)
        field_ref[at, :] = field
        image_ref[at, :] = image
        new = (field * field, field * image, image * image)
        return tuple(old + folded(value) for old, value in zip(sums, new))

    blank = jnp.zeros((8, LANES), F32)
    sums = lax.fori_loop(0, GATHERED, place, (blank, blank, blank), unroll=True)
    norm, cross, square = (over_rows(value) for value in sums)
    guess = jnp.where(square > 0.0, cross / jnp.where(square > 0.0, square, 1.0), 0.0)

    def apart(index, sums):
        at = pl.ds(pl.multiple_of(index * MICS, MICS), MICS)
        image = image_ref[at, :]
        left = field_ref[at, :] - guess * image
        return sums[0] + folded(left * left), sums[1] + folded(left * image)

    sums = lax.fori_loop(0, GATHERED, apart, (blank, blank), unroll=True)
    left_norm, left_cross = (over_rows(value) for value in sums)
    extra = rows_of(norm, cross, square, guess, left_norm, left_cross)
    out_ref[:, PACKED:, :] = jnp.broadcast_to(extra[None], (MID_SIZE, EXTRA, LANES))

    def some_rows(index, carry):
        send_rows(out_ref, index, high_ref, low_ref, weights_ref)
        return carry

    lax.fori_loop(0, ROWS // STEP, some_rows, 0, unroll=True)


def direction_kernel(got_ref, field_ref, image_ref, keep_ref, norm_ref, send_ref):
    norm, cross, square, guess, left_norm, left_cross = (
        got_ref[:, PACKED + i, :] for i in range(6)
    )
    norm = over_rows(norm)
    alpha = norm / over_rows(cross)
    off = guess - alpha
    norm_next = over_rows(left_norm + 2.0 * off * left_cross + off * off * square)
    beta = norm_next / norm
    field, image = widen(field_ref[...]), image_ref[...]
    again = unpack(jnp.sum(got_ref[:, :PACKED, :], axis=0)) + SHIFT * image
    residual = field - alpha * image
    direction = residual + beta * field
    turned = image - alpha * again + beta * image
    keep_ref[0] = alpha * field
    keep_ref[1] = residual
    keep_ref[2] = direction
    keep_ref[3] = turned
    norm_ref[...] = rows_of(norm_next)
    along = over_rows(direction * turned)
    send_ref[...] = jnp.broadcast_to(along[None], send_ref.shape)


def relay_kernel(got_ref, send_ref):
    total = jnp.sum(got_ref[...], axis=0)
    send_ref[...] = jnp.broadcast_to(total[None], send_ref.shape)


def end_kernel(got_ref, norm_ref, keep_ref, solution_ref, residual_ref):
    along = jnp.sum(got_ref[...], axis=0)
    alpha = norm_ref[0:1] / along
    solution_ref[...] = (keep_ref[0] + alpha * keep_ref[2])[:, :FRAMES]
    residual_ref[...] = (keep_ref[1] - alpha * keep_ref[3])[:, :FRAMES]


def call(kernel, outs, **more):
    return pl.pallas_call(
        kernel,
        out_shape=tuple(jax.ShapeDtypeStruct(shape, dtype) for shape, dtype in outs),
        compiler_params=PARAMS,
        **more,
    )


def local(right_side, positions, wavenumber):
    field = right_side.T
    block = (MICS, LANES)

    def exchange(value, axes):
        groups = groups_of(axes)
        return lax.all_to_all(value, tuple(AXES), 0, 0, axis_index_groups=groups)

    def gather(value):
        both = lax.all_gather(exchange(value, FAR), "core")
        return both.reshape((GATHERED,) + value.shape[1:])

    scalar = pl.BlockSpec(memory_space=pltpu.SMEM)
    vector = pl.BlockSpec(memory_space=pltpu.VMEM)
    to_cols, points = call(
        start_kernel,
        [((FAR_SIZE, PACKED + EXTRA, LANES), F32), ((MID_SIZE, EXTRA, LANES), F32)],
    )(field, positions)
    col_blocks = gather(to_cols)
    row_points = exchange(points, MID)

    partial, high, low = call(
        first_kernel,
        [((MID_SIZE, PACKED, LANES), F32), ((ROWS, COLS), BF16), ((ROWS, COLS), BF16)],
        in_specs=[vector, vector, scalar],
        scratch_shapes=[
            pltpu.VMEM((COLS, 2 * LANES), BF16),
            pltpu.VMEM((DEPTH, COLS), BF16),
            pltpu.VMEM((ROWS, DEPTH), BF16),
        ],
    )(col_blocks, row_points, wavenumber)
    image, to_cols = call(image_kernel, [(block, F32), ((FAR_SIZE, PACKED, LANES), F32)])(
        exchange(partial, MID), field
    )
    (partial,) = call(
        second_kernel,
        [((MID_SIZE, PACKED + EXTRA, LANES), F32)],
        scratch_shapes=[
            pltpu.VMEM((COLS, 2 * LANES), BF16),
            pltpu.VMEM((COLS, LANES), F32),
            pltpu.VMEM((COLS, LANES), F32),
        ],
    )(gather(to_cols), col_blocks, high, low)
    keep, norm_next, send = call(
        direction_kernel,
        [((4,) + block, F32), ((EXTRA, LANES), F32), ((FIRST_SIZE, 1, LANES), F32)],
    )(exchange(partial, MID), field, image)
    (send,) = call(relay_kernel, [((LAST_SIZE, 1, LANES), F32)])(exchange(send, FIRST))
    solution_field, residual = call(
        end_kernel, [((MICS, FRAMES), F32), ((MICS, FRAMES), F32)]
    )(exchange(send, LAST), norm_next, keep)
    return solution_field.T, residual.T


def solution(mesh):
    fine = Mesh(mesh.devices.reshape(tuple(AXES.values())), tuple(AXES))
    where = P(None, tuple(AXES))
    return jax.shard_map(
        local,
        mesh=fine,
        in_specs=(where, where, P()),
        out_specs=(where, where),
        check_vma=False,
    )
```

```python
import math

import jax
import jax.numpy as jnp
import numpy as np
from jax import lax
from jax.experimental import pallas as pl
from jax.experimental.pallas import tpu as pltpu
from jax.sharding import Mesh
from jax.sharding import PartitionSpec as P

LANES = 128
MICS = 64
FRAMES = 96
PACKED = 48
EXTRA = 8
STEP = 256
DEPTH = 64
SHIFT = 0.01
BF16 = jnp.bfloat16
F32 = jnp.float32
AXES = {"z_far": 4, "z_near": 2, "y_far": 4, "y_near": 2, "x": 4, "core": 2}
FAR, FAR_SIZE = {"z_far": 2, "y_far": 2}, 16
MID, MID_SIZE = {"z_near": 0, "y_near": 0, "x": 2}, 16
FIRST, FIRST_SIZE = {"z_far": 2, "z_near": 0, "core": 0}, 16
LAST, LAST_SIZE = {"y_far": 2, "y_near": 0, "x": 2}, 32
GATHERED = 2 * FAR_SIZE
ROWS, COLS = MID_SIZE * MICS, GATHERED * MICS
SINC = (
    0.9999999403953552,
    -6.579718112945557,
    12.987034797668457,
    -12.193572998046875,
    6.579925060272217,
    -1.9848603010177612,
)
PARAMS = pltpu.CompilerParams(vmem_limit_bytes=24 * 1024 * 1024)


def groups_of(axes):
    places = np.arange(math.prod(AXES.values())).reshape(tuple(AXES.values()))
    names = list(AXES)
    for name, first in axes.items():
        places = np.roll(places, -first, names.index(name))
    members = math.prod(AXES[name] for name in axes)
    places = np.moveaxis(places, [names.index(name) for name in axes], range(-len(axes), 0))
    return places.reshape(-1, members).tolist()


def dot(left, right):
    return lax.dot_general(left, right, (((1,), (0,)), ((), ())), preferred_element_type=F32)


def rounded(value):
    return value.astype(BF16).astype(F32)


def halves(value):
    high = value.astype(BF16)
    return high, (value - high.astype(F32)).astype(BF16)


def widen(value):
    blank = jnp.zeros((value.shape[0], LANES - value.shape[1]), F32)
    return jnp.concatenate([value, blank], axis=1)


def pack(value):
    tail = value[PACKED:]
    third = FRAMES // 3
    spare = [tail[:, i * third : (i + 1) * third] for i in range(3)]
    return jnp.concatenate([value[:PACKED, :FRAMES], jnp.concatenate(spare, axis=0)], axis=1)


def unpack(block):
    spare = block[:, FRAMES:]
    tail = [spare[i * 16 : (i + 1) * 16] for i in range(3)]
    top = widen(block[:, :FRAMES])
    bottom = widen(jnp.concatenate(tail, axis=1))
    return jnp.concatenate([top, bottom], axis=0)


def rows_of(*rows):
    blank = jnp.zeros((EXTRA - len(rows), LANES), F32)
    return jnp.concatenate(list(rows) + [blank], axis=0)


def over_rows(value):
    return jnp.sum(value, axis=0, keepdims=True)


def start_kernel(both_ref, col_ref, row_ref):
    points = both_ref[MICS:]
    block = jnp.concatenate([pack(both_ref[:MICS]), points], axis=0)
    col_ref[...] = jnp.broadcast_to(block[None], col_ref.shape)
    row_ref[...] = jnp.broadcast_to(points[None], row_ref.shape)


def factors(points, wave, of_rows):
    scaled = points * (wave * (0.5 / math.pi))
    squares = over_rows(scaled * scaled)

    def thirds(value):
        one = rounded(value)
        two = rounded(value - one)
        return one, two, rounded(value - one - two)

    one, two, three = thirds(scaled)
    ones = jnp.ones_like(squares)
    if of_rows:
        rows = [one, one, two, two, one, three]
        rest = list(thirds(squares)) + [ones] * 3
    else:
        rows = [-2.0 * v for v in (one, two, one, two, three, one)]
        rest = [ones] * 3 + list(thirds(squares))
    blank = jnp.zeros((DEPTH - 6 * EXTRA - 6, squares.shape[1]), F32)
    return jnp.concatenate(rows + rest + [blank], axis=0)


def points_of(ref, count, first):
    tiles = [ref[i, first : first + EXTRA, :MICS] for i in range(count)]
    return jnp.concatenate(tiles, axis=1)


def sinc_of(turns2):
    turns2 = jnp.maximum(turns2, 1e-12)
    inverse = lax.rsqrt(turns2)
    turns = turns2 * inverse
    part = turns - lax.round(turns, lax.RoundingMethod.TO_NEAREST_EVEN)
    square = part * part
    value = SINC[-1] * square + SINC[-2]
    for factor in SINC[-3::-1]:
        value = value * square + factor
    return value * (part * inverse)


def put_weights(weights_ref, index, value):
    at = pl.ds(pl.multiple_of(index * MICS, MICS), MICS)
    high, low = halves(value)
    weights_ref[at, :LANES] = high
    weights_ref[at, LANES:] = low


def send_rows(out_ref, index, high_ref, low_ref, weights_ref):
    at = pl.ds(pl.multiple_of(index * STEP, STEP), STEP)
    both = dot(high_ref[at, :], weights_ref[...])
    rest = dot(low_ref[at, :], weights_ref[:, :LANES])
    total = both[:, :LANES] + both[:, LANES:] + rest
    for i in range(STEP // MICS):
        packed = pack(total[i * MICS : (i + 1) * MICS])
        out_ref[index * (STEP // MICS) + i, :PACKED, :] = packed


def prepare_kernel(col_ref, wave_ref, weights_ref, col_f):
    def place(index, carry):
        put_weights(weights_ref, index, unpack(col_ref[index, :PACKED, :]))
        return carry

    lax.fori_loop(0, GATHERED, place, 0, unroll=True)
    cols = points_of(col_ref, GATHERED, PACKED)
    col_f[...] = factors(cols, wave_ref[0], False).astype(BF16)


def first_kernel(
    weights_ref, col_f, row_ref, wave_ref, out_ref, high_ref, low_ref, row_f
):
    rows = points_of(row_ref, MID_SIZE, 0)
    row_f[...] = factors(rows, wave_ref[0], True).T.astype(BF16)

    def some_rows(index, carry):
        at = pl.ds(pl.multiple_of(index * STEP, STEP), STEP)
        left = row_f[at, :]
        for first in range(0, COLS, STEP):
            cols = slice(first, first + STEP)
            high, low = halves(sinc_of(dot(left, col_f[:, cols])))
            high_ref[at, cols] = high
            low_ref[at, cols] = low
        send_rows(out_ref, index, high_ref, low_ref, weights_ref)
        return carry

    lax.fori_loop(0, ROWS // STEP, some_rows, 0, unroll=True)


def image_kernel(got_ref, field_ref, image_ref, send_ref):
    image = unpack(jnp.sum(got_ref[...], axis=0)) + SHIFT * widen(field_ref[...])
    image_ref[...] = image
    send_ref[...] = jnp.broadcast_to(pack(image)[None], send_ref.shape)


def second_kernel(
    got_ref, col_ref, high_ref, low_ref, out_ref, weights_ref, field_ref, image_ref
):
    def folded(value):
        return jnp.sum(value.reshape(-1, 8, LANES), axis=0)

    def place(index, sums):
        at = pl.ds(pl.multiple_of(index * MICS, MICS), MICS)
        image = unpack(got_ref[index])
        field = unpack(col_ref[index, :PACKED, :])
        put_weights(weights_ref, index, image)
        field_ref[at, :] = field
        image_ref[at, :] = image
        new = (field * field, field * image, image * image)
        return tuple(old + folded(value) for old, value in zip(sums, new))

    blank = jnp.zeros((8, LANES), F32)
    sums = lax.fori_loop(0, GATHERED, place, (blank, blank, blank), unroll=True)
    norm, cross, square = (over_rows(value) for value in sums)
    guess = jnp.where(square > 0.0, cross / jnp.where(square > 0.0, square, 1.0), 0.0)

    def apart(index, sums):
        at = pl.ds(pl.multiple_of(index * MICS, MICS), MICS)
        image = image_ref[at, :]
        left = field_ref[at, :] - guess * image
        return sums[0] + folded(left * left), sums[1] + folded(left * image)

    sums = lax.fori_loop(0, GATHERED, apart, (blank, blank), unroll=True)
    left_norm, left_cross = (over_rows(value) for value in sums)
    extra = rows_of(norm, cross, square, guess, left_norm, left_cross)
    out_ref[:, PACKED:, :] = jnp.broadcast_to(extra[None], (MID_SIZE, EXTRA, LANES))

    def some_rows(index, carry):
        send_rows(out_ref, index, high_ref, low_ref, weights_ref)
        return carry

    lax.fori_loop(0, ROWS // STEP, some_rows, 0, unroll=True)


def direction_kernel(got_ref, field_ref, image_ref, keep_ref, norm_ref, send_ref):
    norm, cross, square, guess, left_norm, left_cross = (
        got_ref[:, PACKED + i, :] for i in range(6)
    )
    norm = over_rows(norm)
    alpha = norm / over_rows(cross)
    off = guess - alpha
    norm_next = over_rows(left_norm + 2.0 * off * left_cross + off * off * square)
    beta = norm_next / norm
    field, image = widen(field_ref[...]), image_ref[...]
    again = unpack(jnp.sum(got_ref[:, :PACKED, :], axis=0)) + SHIFT * image
    residual = field - alpha * image
    direction = residual + beta * field
    turned = image - alpha * again + beta * image
    keep_ref[0] = alpha * field
    keep_ref[1] = residual
    keep_ref[2] = direction
    keep_ref[3] = turned
    norm_ref[...] = rows_of(norm_next)
    along = over_rows(direction * turned)
    send_ref[...] = jnp.broadcast_to(along[None], send_ref.shape)


def relay_kernel(got_ref, send_ref):
    total = jnp.sum(got_ref[...], axis=0)
    send_ref[...] = jnp.broadcast_to(total[None], send_ref.shape)


def end_kernel(got_ref, norm_ref, keep_ref, solution_ref, residual_ref):
    along = jnp.sum(got_ref[...], axis=0)
    alpha = norm_ref[0:1] / along
    solution_ref[...] = (keep_ref[0] + alpha * keep_ref[2])[:, :FRAMES]
    residual_ref[...] = (keep_ref[1] - alpha * keep_ref[3])[:, :FRAMES]


def call(kernel, outs, **more):
    return pl.pallas_call(
        kernel,
        out_shape=tuple(jax.ShapeDtypeStruct(shape, dtype) for shape, dtype in outs),
        compiler_params=PARAMS,
        **more,
    )


def local(right_side, positions, wavenumber):
    field = right_side.T
    block = (MICS, LANES)

    def exchange(value, axes):
        groups = groups_of(axes)
        return lax.all_to_all(value, tuple(AXES), 0, 0, axis_index_groups=groups)

    def gather(value):
        both = lax.all_gather(exchange(value, FAR), "core")
        return both.reshape((GATHERED,) + value.shape[1:])

    scalar = pl.BlockSpec(memory_space=pltpu.SMEM)
    vector = pl.BlockSpec(memory_space=pltpu.VMEM)
    spare = jnp.pad(positions, ((0, EXTRA - 3), (0, LANES - MICS)))
    to_cols, points = call(
        start_kernel,
        [((FAR_SIZE, PACKED + EXTRA, LANES), F32), ((MID_SIZE, EXTRA, LANES), F32)],
    )(jnp.concatenate([widen(field), spare], axis=0))
    col_blocks = gather(to_cols)
    row_points = exchange(points, MID)

    weights, col_factors = call(
        prepare_kernel,
        [((COLS, 2 * LANES), BF16), ((DEPTH, COLS), BF16)],
        in_specs=[vector, scalar],
    )(col_blocks, wavenumber)
    partial, high, low = call(
        first_kernel,
        [((MID_SIZE, PACKED, LANES), F32), ((ROWS, COLS), BF16), ((ROWS, COLS), BF16)],
        in_specs=[vector, vector, vector, scalar],
        scratch_shapes=[pltpu.VMEM((ROWS, DEPTH), BF16)],
    )(weights, col_factors, row_points, wavenumber)
    image, to_cols = call(image_kernel, [(block, F32), ((FAR_SIZE, PACKED, LANES), F32)])(
        exchange(partial, MID), field
    )
    (partial,) = call(
        second_kernel,
        [((MID_SIZE, PACKED + EXTRA, LANES), F32)],
        scratch_shapes=[
            pltpu.VMEM((COLS, 2 * LANES), BF16),
            pltpu.VMEM((COLS, LANES), F32),
            pltpu.VMEM((COLS, LANES), F32),
        ],
    )(gather(to_cols), col_blocks, high, low)
    keep, norm_next, send = call(
        direction_kernel,
        [((4,) + block, F32), ((EXTRA, LANES), F32), ((FIRST_SIZE, 1, LANES), F32)],
    )(exchange(partial, MID), field, image)
    (send,) = call(relay_kernel, [((LAST_SIZE, 1, LANES), F32)])(exchange(send, FIRST))
    solution_field, residual = call(
        end_kernel, [((MICS, FRAMES), F32), ((MICS, FRAMES), F32)]
    )(exchange(send, LAST), norm_next, keep)
    return solution_field.T, residual.T


def solution(mesh):
    fine = Mesh(mesh.devices.reshape(tuple(AXES.values())), tuple(AXES))
    where = P(None, tuple(AXES))
    return jax.shard_map(
        local,
        mesh=fine,
        in_specs=(where, where, P()),
        out_specs=(where, where),
        check_vma=False,
    )
```

```python
import math

import jax
import jax.numpy as jnp
import numpy as np
from jax import lax
from jax.experimental import pallas as pl
from jax.experimental.pallas import tpu as pltpu
from jax.sharding import Mesh
from jax.sharding import PartitionSpec as P

LANES = 128
MICS = 64
FRAMES = 96
PACKED = 48
EXTRA = 8
STEP = 512
DEPTH = 64
SHIFT = 0.01
BF16 = jnp.bfloat16
F32 = jnp.float32
AXES = {"z_far": 4, "z_near": 2, "y_far": 4, "y_near": 2, "x": 4, "core": 2}
FAR, FAR_SIZE = {"z_far": 2, "y_far": 2}, 16
MID, MID_SIZE = {"z_near": 1, "y_near": 1, "x": 2}, 16
FIRST, FIRST_SIZE = {"z_far": 2, "z_near": 0, "core": 1}, 16
LAST, LAST_SIZE = {"y_far": 2, "y_near": 0, "x": 2}, 32
GATHERED = 2 * FAR_SIZE
ROWS, COLS = MID_SIZE * MICS, GATHERED * MICS
SINC = (
    0.9999999403953552,
    -6.579718112945557,
    12.987034797668457,
    -12.193572998046875,
    6.579925060272217,
    -1.9848603010177612,
)
PARAMS = pltpu.CompilerParams(vmem_limit_bytes=24 * 1024 * 1024)


def groups_of(axes):
    places = np.arange(math.prod(AXES.values())).reshape(tuple(AXES.values()))
    names = list(AXES)
    for name, first in axes.items():
        places = np.roll(places, -first, names.index(name))
    members = math.prod(AXES[name] for name in axes)
    places = np.moveaxis(places, [names.index(name) for name in axes], range(-len(axes), 0))
    return places.reshape(-1, members).tolist()


def dot(left, right):
    return lax.dot_general(left, right, (((1,), (0,)), ((), ())), preferred_element_type=F32)


def rounded(value):
    return value.astype(BF16).astype(F32)


def halves(value):
    high = value.astype(BF16)
    return high, (value - high.astype(F32)).astype(BF16)


def widen(value):
    blank = jnp.zeros((value.shape[0], LANES - value.shape[1]), F32)
    return jnp.concatenate([value, blank], axis=1)


def pack(value):
    tail = value[PACKED:]
    third = FRAMES // 3
    spare = [tail[:, i * third : (i + 1) * third] for i in range(3)]
    return jnp.concatenate([value[:PACKED, :FRAMES], jnp.concatenate(spare, axis=0)], axis=1)


def unpack(block):
    spare = block[:, FRAMES:]
    tail = [spare[i * 16 : (i + 1) * 16] for i in range(3)]
    top = widen(block[:, :FRAMES])
    bottom = widen(jnp.concatenate(tail, axis=1))
    return jnp.concatenate([top, bottom], axis=0)


def rows_of(*rows):
    blank = jnp.zeros((EXTRA - len(rows), LANES), F32)
    return jnp.concatenate(list(rows) + [blank], axis=0)


def over_rows(value):
    return jnp.sum(value, axis=0, keepdims=True)


def start_kernel(both_ref, col_ref, row_ref):
    points = both_ref[MICS:]
    block = jnp.concatenate([pack(both_ref[:MICS]), points], axis=0)
    col_ref[...] = jnp.broadcast_to(block[None], col_ref.shape)
    row_ref[...] = jnp.broadcast_to(points[None], row_ref.shape)


def factors(points, wave, of_rows):
    scaled = points * (wave * (0.5 / math.pi))
    squares = over_rows(scaled * scaled)

    def thirds(value):
        one = rounded(value)
        two = rounded(value - one)
        return one, two, rounded(value - one - two)

    one, two, three = thirds(scaled)
    ones = jnp.ones_like(squares)
    if of_rows:
        rows = [one, one, two, two, one, three]
        rest = list(thirds(squares)) + [ones] * 3
    else:
        rows = [-2.0 * v for v in (one, two, one, two, three, one)]
        rest = [ones] * 3 + list(thirds(squares))
    blank = jnp.zeros((DEPTH - 6 * EXTRA - 6, squares.shape[1]), F32)
    return jnp.concatenate(rows + rest + [blank], axis=0)


def points_of(ref, count, first):
    tiles = [ref[i, first : first + EXTRA, :MICS] for i in range(count)]
    return jnp.concatenate(tiles, axis=1)


def sinc_of(turns2):
    turns2 = jnp.maximum(turns2, 1e-12)
    inverse = lax.rsqrt(turns2)
    turns = turns2 * inverse
    part = turns - lax.round(turns, lax.RoundingMethod.TO_NEAREST_EVEN)
    square = part * part
    value = SINC[-1] * square + SINC[-2]
    for factor in SINC[-3::-1]:
        value = value * square + factor
    return value * (part * inverse)


def put_weights(weights_ref, index, value):
    at = pl.ds(pl.multiple_of(index * MICS, MICS), MICS)
    high, low = halves(value)
    weights_ref[at, :LANES] = high
    weights_ref[at, LANES:] = low


def send_rows(out_ref, index, high_ref, low_ref, weights_ref):
    at = pl.ds(pl.multiple_of(index * STEP, STEP), STEP)
    both = dot(high_ref[at, :], weights_ref[...])
    rest = dot(low_ref[at, :], weights_ref[:, :LANES])
    total = both[:, :LANES] + both[:, LANES:] + rest
    for i in range(STEP // MICS):
        packed = pack(total[i * MICS : (i + 1) * MICS])
        out_ref[index * (STEP // MICS) + i, :PACKED, :] = packed


def prepare_kernel(col_ref, wave_ref, weights_ref, col_f):
    def place(index, carry):
        put_weights(weights_ref, index, unpack(col_ref[index, :PACKED, :]))
        return carry

    lax.fori_loop(0, GATHERED, place, 0, unroll=True)
    cols = points_of(col_ref, GATHERED, PACKED)
    col_f[...] = factors(cols, wave_ref[0], False).astype(BF16)


def first_kernel(
    weights_ref, col_f, row_ref, wave_ref, out_ref, high_ref, low_ref, row_f
):
    rows = points_of(row_ref, MID_SIZE, 0)
    row_f[...] = factors(rows, wave_ref[0], True).T.astype(BF16)

    def some_rows(index, carry):
        at = pl.ds(pl.multiple_of(index * STEP, STEP), STEP)
        left = row_f[at, :]
        for first in range(0, COLS, STEP):
            cols = slice(first, first + STEP)
            high, low = halves(sinc_of(dot(left, col_f[:, cols])))
            high_ref[at, cols] = high
            low_ref[at, cols] = low
        send_rows(out_ref, index, high_ref, low_ref, weights_ref)
        return carry

    lax.fori_loop(0, ROWS // STEP, some_rows, 0, unroll=True)


def image_kernel(got_ref, field_ref, image_ref, send_ref):
    image = unpack(jnp.sum(got_ref[...], axis=0)) + SHIFT * widen(field_ref[...])
    image_ref[...] = image
    send_ref[...] = jnp.broadcast_to(pack(image)[None], send_ref.shape)


def second_kernel(
    got_ref, col_ref, high_ref, low_ref, out_ref, weights_ref, field_ref, image_ref
):
    def folded(value):
        return jnp.sum(value.reshape(-1, 8, LANES), axis=0)

    def place(index, sums):
        at = pl.ds(pl.multiple_of(index * MICS, MICS), MICS)
        image = unpack(got_ref[index])
        field = unpack(col_ref[index, :PACKED, :])
        put_weights(weights_ref, index, image)
        field_ref[at, :] = field
        image_ref[at, :] = image
        new = (field * field, field * image, image * image)
        return tuple(old + folded(value) for old, value in zip(sums, new))

    blank = jnp.zeros((8, LANES), F32)
    sums = lax.fori_loop(0, GATHERED, place, (blank, blank, blank), unroll=True)
    norm, cross, square = (over_rows(value) for value in sums)
    guess = jnp.where(square > 0.0, cross / jnp.where(square > 0.0, square, 1.0), 0.0)

    def apart(index, sums):
        at = pl.ds(pl.multiple_of(index * MICS, MICS), MICS)
        image = image_ref[at, :]
        left = field_ref[at, :] - guess * image
        return sums[0] + folded(left * left), sums[1] + folded(left * image)

    sums = lax.fori_loop(0, GATHERED, apart, (blank, blank), unroll=True)
    left_norm, left_cross = (over_rows(value) for value in sums)
    extra = rows_of(norm, cross, square, guess, left_norm, left_cross)
    out_ref[:, PACKED:, :] = jnp.broadcast_to(extra[None], (MID_SIZE, EXTRA, LANES))

    def some_rows(index, carry):
        send_rows(out_ref, index, high_ref, low_ref, weights_ref)
        return carry

    lax.fori_loop(0, ROWS // STEP, some_rows, 0, unroll=True)


def direction_kernel(got_ref, field_ref, image_ref, keep_ref, norm_ref, send_ref):
    norm, cross, square, guess, left_norm, left_cross = (
        got_ref[:, PACKED + i, :] for i in range(6)
    )
    norm = over_rows(norm)
    alpha = norm / over_rows(cross)
    off = guess - alpha
    norm_next = over_rows(left_norm + 2.0 * off * left_cross + off * off * square)
    beta = norm_next / norm
    field, image = widen(field_ref[...]), image_ref[...]
    again = unpack(jnp.sum(got_ref[:, :PACKED, :], axis=0)) + SHIFT * image
    residual = field - alpha * image
    direction = residual + beta * field
    turned = image - alpha * again + beta * image
    keep_ref[0] = alpha * field
    keep_ref[1] = residual
    keep_ref[2] = direction
    keep_ref[3] = turned
    norm_ref[...] = rows_of(norm_next)
    along = over_rows(direction * turned)
    send_ref[...] = jnp.broadcast_to(along[None], send_ref.shape)


def relay_kernel(got_ref, send_ref):
    total = jnp.sum(got_ref[...], axis=0)
    send_ref[...] = jnp.broadcast_to(total[None], send_ref.shape)


def end_kernel(got_ref, norm_ref, keep_ref, solution_ref, residual_ref):
    along = jnp.sum(got_ref[...], axis=0)
    alpha = norm_ref[0:1] / along
    solution_ref[...] = (keep_ref[0] + alpha * keep_ref[2])[:, :FRAMES]
    residual_ref[...] = (keep_ref[1] - alpha * keep_ref[3])[:, :FRAMES]


def call(kernel, outs, **more):
    return pl.pallas_call(
        kernel,
        out_shape=tuple(jax.ShapeDtypeStruct(shape, dtype) for shape, dtype in outs),
        compiler_params=PARAMS,
        **more,
    )


def local(right_side, positions, wavenumber):
    field = right_side.T
    block = (MICS, LANES)

    def exchange(value, axes):
        groups = groups_of(axes)
        return lax.all_to_all(value, tuple(AXES), 0, 0, axis_index_groups=groups)

    def gather(value):
        both = lax.all_gather(exchange(value, FAR), "core")
        return both.reshape((GATHERED,) + value.shape[1:])

    scalar = pl.BlockSpec(memory_space=pltpu.SMEM)
    vector = pl.BlockSpec(memory_space=pltpu.VMEM)
    spare = jnp.pad(positions, ((0, EXTRA - 3), (0, LANES - MICS)))
    to_cols, points = call(
        start_kernel,
        [((FAR_SIZE, PACKED + EXTRA, LANES), F32), ((MID_SIZE, EXTRA, LANES), F32)],
    )(jnp.concatenate([widen(field), spare], axis=0))
    col_blocks = gather(to_cols)
    row_points = exchange(points, MID)

    weights, col_factors = call(
        prepare_kernel,
        [((COLS, 2 * LANES), BF16), ((DEPTH, COLS), BF16)],
        in_specs=[vector, scalar],
    )(col_blocks, wavenumber)
    partial, high, low = call(
        first_kernel,
        [((MID_SIZE, PACKED, LANES), F32), ((ROWS, COLS), BF16), ((ROWS, COLS), BF16)],
        in_specs=[vector, vector, vector, scalar],
        scratch_shapes=[pltpu.VMEM((ROWS, DEPTH), BF16)],
    )(weights, col_factors, row_points, wavenumber)
    image, to_cols = call(image_kernel, [(block, F32), ((FAR_SIZE, PACKED, LANES), F32)])(
        exchange(partial, MID), field
    )
    (partial,) = call(
        second_kernel,
        [((MID_SIZE, PACKED + EXTRA, LANES), F32)],
        scratch_shapes=[
            pltpu.VMEM((COLS, 2 * LANES), BF16),
            pltpu.VMEM((COLS, LANES), F32),
            pltpu.VMEM((COLS, LANES), F32),
        ],
    )(gather(to_cols), col_blocks, high, low)
    keep, norm_next, send = call(
        direction_kernel,
        [((4,) + block, F32), ((EXTRA, LANES), F32), ((FIRST_SIZE, 1, LANES), F32)],
    )(exchange(partial, MID), field, image)
    (send,) = call(relay_kernel, [((LAST_SIZE, 1, LANES), F32)])(exchange(send, FIRST))
    solution_field, residual = call(
        end_kernel, [((MICS, FRAMES), F32), ((MICS, FRAMES), F32)]
    )(exchange(send, LAST), norm_next, keep)
    return solution_field.T, residual.T


def solution(mesh):
    fine = Mesh(mesh.devices.reshape(tuple(AXES.values())), tuple(AXES))
    where = P(None, tuple(AXES))
    return jax.shard_map(
        local,
        mesh=fine,
        in_specs=(where, where, P()),
        out_specs=(where, where),
        check_vma=False,
    )
```

```python
import math

import jax
import jax.numpy as jnp
import numpy as np
from jax import lax
from jax.experimental import pallas as pl
from jax.experimental.pallas import tpu as pltpu
from jax.sharding import Mesh
from jax.sharding import PartitionSpec as P

LANES = 128
MICS = 64
FRAMES = 96
PACKED = 48
EXTRA = 8
STEP = 1024
DEPTH = 64
SHIFT = 0.01
BF16 = jnp.bfloat16
F32 = jnp.float32
AXES = {"z_far": 4, "z_near": 2, "y_far": 4, "y_near": 2, "x": 4, "core": 2}
FAR, FAR_SIZE = {"z_far": 2, "y_far": 2}, 16
MID, MID_SIZE = {"z_near": 1, "y_near": 1, "x": 2}, 16
FIRST, FIRST_SIZE = {"z_far": 2, "z_near": 0, "core": 1}, 16
LAST, LAST_SIZE = {"y_far": 2, "y_near": 0, "x": 2}, 32
GATHERED = 2 * FAR_SIZE
ROWS, COLS = MID_SIZE * MICS, GATHERED * MICS
SINC = (
    0.9999999403953552,
    -6.579718112945557,
    12.987034797668457,
    -12.193572998046875,
    6.579925060272217,
    -1.9848603010177612,
)
PARAMS = pltpu.CompilerParams(vmem_limit_bytes=24 * 1024 * 1024)


def groups_of(axes):
    places = np.arange(math.prod(AXES.values())).reshape(tuple(AXES.values()))
    names = list(AXES)
    for name, first in axes.items():
        places = np.roll(places, -first, names.index(name))
    members = math.prod(AXES[name] for name in axes)
    places = np.moveaxis(places, [names.index(name) for name in axes], range(-len(axes), 0))
    return places.reshape(-1, members).tolist()


def dot(left, right):
    return lax.dot_general(left, right, (((1,), (0,)), ((), ())), preferred_element_type=F32)


def rounded(value):
    return value.astype(BF16).astype(F32)


def halves(value):
    high = value.astype(BF16)
    return high, (value - high.astype(F32)).astype(BF16)


def widen(value):
    blank = jnp.zeros((value.shape[0], LANES - value.shape[1]), F32)
    return jnp.concatenate([value, blank], axis=1)


def pack(value):
    tail = value[PACKED:]
    third = FRAMES // 3
    spare = [tail[:, i * third : (i + 1) * third] for i in range(3)]
    return jnp.concatenate([value[:PACKED, :FRAMES], jnp.concatenate(spare, axis=0)], axis=1)


def unpack(block):
    spare = block[:, FRAMES:]
    tail = [spare[i * 16 : (i + 1) * 16] for i in range(3)]
    top = widen(block[:, :FRAMES])
    bottom = widen(jnp.concatenate(tail, axis=1))
    return jnp.concatenate([top, bottom], axis=0)


def rows_of(*rows):
    blank = jnp.zeros((EXTRA - len(rows), LANES), F32)
    return jnp.concatenate(list(rows) + [blank], axis=0)


def over_rows(value):
    return jnp.sum(value, axis=0, keepdims=True)


def start_kernel(both_ref, col_ref, row_ref):
    points = both_ref[MICS:]
    block = jnp.concatenate([pack(both_ref[:MICS]), points], axis=0)
    col_ref[...] = jnp.broadcast_to(block[None], col_ref.shape)
    row_ref[...] = jnp.broadcast_to(points[None], row_ref.shape)


def factors(points, wave, of_rows):
    scaled = points * (wave * (0.5 / math.pi))
    squares = over_rows(scaled * scaled)

    def thirds(value):
        one = rounded(value)
        two = rounded(value - one)
        return one, two, rounded(value - one - two)

    one, two, three = thirds(scaled)
    ones = jnp.ones_like(squares)
    if of_rows:
        rows = [one, one, two, two, one, three]
        rest = list(thirds(squares)) + [ones] * 3
    else:
        rows = [-2.0 * v for v in (one, two, one, two, three, one)]
        rest = [ones] * 3 + list(thirds(squares))
    blank = jnp.zeros((DEPTH - 6 * EXTRA - 6, squares.shape[1]), F32)
    return jnp.concatenate(rows + rest + [blank], axis=0)


def points_of(ref, count, first):
    tiles = [ref[i, first : first + EXTRA, :MICS] for i in range(count)]
    return jnp.concatenate(tiles, axis=1)


def sinc_of(turns2):
    turns2 = jnp.maximum(turns2, 1e-12)
    inverse = lax.rsqrt(turns2)
    turns = turns2 * inverse
    part = turns - lax.round(turns, lax.RoundingMethod.TO_NEAREST_EVEN)
    square = part * part
    value = SINC[-1] * square + SINC[-2]
    for factor in SINC[-3::-1]:
        value = value * square + factor
    return value * (part * inverse)


def put_weights(weights_ref, index, value):
    at = pl.ds(pl.multiple_of(index * MICS, MICS), MICS)
    high, low = halves(value)
    weights_ref[at, :LANES] = high
    weights_ref[at, LANES:] = low


def send_rows(out_ref, index, high_ref, low_ref, weights_ref):
    at = pl.ds(pl.multiple_of(index * STEP, STEP), STEP)
    both = dot(high_ref[at, :], weights_ref[...])
    rest = dot(low_ref[at, :], weights_ref[:, :LANES])
    total = both[:, :LANES] + both[:, LANES:] + rest
    for i in range(STEP // MICS):
        packed = pack(total[i * MICS : (i + 1) * MICS])
        out_ref[index * (STEP // MICS) + i, :PACKED, :] = packed


def prepare_kernel(col_ref, wave_ref, weights_ref, col_f):
    def place(index, carry):
        put_weights(weights_ref, index, unpack(col_ref[index, :PACKED, :]))
        return carry

    lax.fori_loop(0, GATHERED, place, 0, unroll=True)
    cols = points_of(col_ref, GATHERED, PACKED)
    col_f[...] = factors(cols, wave_ref[0], False).astype(BF16)


def first_kernel(
    weights_ref, col_f, row_ref, wave_ref, out_ref, high_ref, low_ref, row_f
):
    rows = points_of(row_ref, MID_SIZE, 0)
    row_f[...] = factors(rows, wave_ref[0], True).T.astype(BF16)

    def some_rows(index, carry):
        at = pl.ds(pl.multiple_of(index * STEP, STEP), STEP)
        left = row_f[at, :]
        for first in range(0, COLS, STEP):
            cols = slice(first, first + STEP)
            high, low = halves(sinc_of(dot(left, col_f[:, cols])))
            high_ref[at, cols] = high
            low_ref[at, cols] = low
        send_rows(out_ref, index, high_ref, low_ref, weights_ref)
        return carry

    lax.fori_loop(0, ROWS // STEP, some_rows, 0, unroll=True)


def image_kernel(got_ref, field_ref, image_ref, send_ref):
    image = unpack(jnp.sum(got_ref[...], axis=0)) + SHIFT * widen(field_ref[...])
    image_ref[...] = image
    send_ref[...] = jnp.broadcast_to(pack(image)[None], send_ref.shape)


def second_kernel(
    got_ref, col_ref, high_ref, low_ref, out_ref, weights_ref, field_ref, image_ref
):
    def folded(value):
        return jnp.sum(value.reshape(-1, 8, LANES), axis=0)

    def place(index, sums):
        at = pl.ds(pl.multiple_of(index * MICS, MICS), MICS)
        image = unpack(got_ref[index])
        field = unpack(col_ref[index, :PACKED, :])
        put_weights(weights_ref, index, image)
        field_ref[at, :] = field
        image_ref[at, :] = image
        new = (field * field, field * image, image * image)
        return tuple(old + folded(value) for old, value in zip(sums, new))

    blank = jnp.zeros((8, LANES), F32)
    sums = lax.fori_loop(0, GATHERED, place, (blank, blank, blank), unroll=True)
    norm, cross, square = (over_rows(value) for value in sums)
    guess = jnp.where(square > 0.0, cross / jnp.where(square > 0.0, square, 1.0), 0.0)

    def apart(index, sums):
        at = pl.ds(pl.multiple_of(index * MICS, MICS), MICS)
        image = image_ref[at, :]
        left = field_ref[at, :] - guess * image
        return sums[0] + folded(left * left), sums[1] + folded(left * image)

    sums = lax.fori_loop(0, GATHERED, apart, (blank, blank), unroll=True)
    left_norm, left_cross = (over_rows(value) for value in sums)
    extra = rows_of(norm, cross, square, guess, left_norm, left_cross)
    out_ref[:, PACKED:, :] = jnp.broadcast_to(extra[None], (MID_SIZE, EXTRA, LANES))

    def some_rows(index, carry):
        send_rows(out_ref, index, high_ref, low_ref, weights_ref)
        return carry

    lax.fori_loop(0, ROWS // STEP, some_rows, 0, unroll=True)


def direction_kernel(got_ref, field_ref, image_ref, keep_ref, norm_ref, send_ref):
    norm, cross, square, guess, left_norm, left_cross = (
        got_ref[:, PACKED + i, :] for i in range(6)
    )
    norm = over_rows(norm)
    alpha = norm / over_rows(cross)
    off = guess - alpha
    norm_next = over_rows(left_norm + 2.0 * off * left_cross + off * off * square)
    beta = norm_next / norm
    field, image = widen(field_ref[...]), image_ref[...]
    again = unpack(jnp.sum(got_ref[:, :PACKED, :], axis=0)) + SHIFT * image
    residual = field - alpha * image
    direction = residual + beta * field
    turned = image - alpha * again + beta * image
    keep_ref[0] = alpha * field
    keep_ref[1] = residual
    keep_ref[2] = direction
    keep_ref[3] = turned
    norm_ref[...] = rows_of(norm_next)
    along = over_rows(direction * turned)
    send_ref[...] = jnp.broadcast_to(along[None], send_ref.shape)


def relay_kernel(got_ref, send_ref):
    total = jnp.sum(got_ref[...], axis=0)
    send_ref[...] = jnp.broadcast_to(total[None], send_ref.shape)


def end_kernel(got_ref, norm_ref, keep_ref, solution_ref, residual_ref):
    along = jnp.sum(got_ref[...], axis=0)
    alpha = norm_ref[0:1] / along
    solution_ref[...] = (keep_ref[0] + alpha * keep_ref[2])[:, :FRAMES]
    residual_ref[...] = (keep_ref[1] - alpha * keep_ref[3])[:, :FRAMES]


def call(kernel, outs, **more):
    return pl.pallas_call(
        kernel,
        out_shape=tuple(jax.ShapeDtypeStruct(shape, dtype) for shape, dtype in outs),
        compiler_params=PARAMS,
        **more,
    )


def local(right_side, positions, wavenumber):
    field = right_side.T
    block = (MICS, LANES)

    def exchange(value, axes):
        groups = groups_of(axes)
        return lax.all_to_all(value, tuple(AXES), 0, 0, axis_index_groups=groups)

    def gather(value):
        both = lax.all_gather(exchange(value, FAR), "core")
        return both.reshape((GATHERED,) + value.shape[1:])

    scalar = pl.BlockSpec(memory_space=pltpu.SMEM)
    vector = pl.BlockSpec(memory_space=pltpu.VMEM)
    spare = jnp.pad(positions, ((0, EXTRA - 3), (0, LANES - MICS)))
    to_cols, points = call(
        start_kernel,
        [((FAR_SIZE, PACKED + EXTRA, LANES), F32), ((MID_SIZE, EXTRA, LANES), F32)],
    )(jnp.concatenate([widen(field), spare], axis=0))
    col_blocks = gather(to_cols)
    row_points = exchange(points, MID)

    weights, col_factors = call(
        prepare_kernel,
        [((COLS, 2 * LANES), BF16), ((DEPTH, COLS), BF16)],
        in_specs=[vector, scalar],
    )(col_blocks, wavenumber)
    partial, high, low = call(
        first_kernel,
        [((MID_SIZE, PACKED, LANES), F32), ((ROWS, COLS), BF16), ((ROWS, COLS), BF16)],
        in_specs=[vector, vector, vector, scalar],
        scratch_shapes=[pltpu.VMEM((ROWS, DEPTH), BF16)],
    )(weights, col_factors, row_points, wavenumber)
    image, to_cols = call(image_kernel, [(block, F32), ((FAR_SIZE, PACKED, LANES), F32)])(
        exchange(partial, MID), field
    )
    (partial,) = call(
        second_kernel,
        [((MID_SIZE, PACKED + EXTRA, LANES), F32)],
        scratch_shapes=[
            pltpu.VMEM((COLS, 2 * LANES), BF16),
            pltpu.VMEM((COLS, LANES), F32),
            pltpu.VMEM((COLS, LANES), F32),
        ],
    )(gather(to_cols), col_blocks, high, low)
    keep, norm_next, send = call(
        direction_kernel,
        [((4,) + block, F32), ((EXTRA, LANES), F32), ((FIRST_SIZE, 1, LANES), F32)],
    )(exchange(partial, MID), field, image)
    (send,) = call(relay_kernel, [((LAST_SIZE, 1, LANES), F32)])(exchange(send, FIRST))
    solution_field, residual = call(
        end_kernel, [((MICS, FRAMES), F32), ((MICS, FRAMES), F32)]
    )(exchange(send, LAST), norm_next, keep)
    return solution_field.T, residual.T


def solution(mesh):
    fine = Mesh(mesh.devices.reshape(tuple(AXES.values())), tuple(AXES))
    where = P(None, tuple(AXES))
    return jax.shard_map(
        local,
        mesh=fine,
        in_specs=(where, where, P()),
        out_specs=(where, where),
        check_vma=False,
    )
```
